32 devices in a mesh: groups: 2 (over y), mp: 4 (over x, core), hidden: 4 (over z).
Axes of the slice: x: 2, y: 2, z: 4, core: 2. Of those that a mesh axis runs over, the one named last changes fastest.
Arguments:
- inputs: bfloat16 [2048, 8192], P(('groups', 'hidden'), 'mp'), parts along dimension 0, as said below
- out_grad: bfloat16 [2048, 16384], P(('groups', 'mp'), 'hidden'), parts along dimension 0, as said below
- weight: float32 [8192, 16384], P('mp', 'hidden'), may hold values from -0.0625 to 0.0625
- noise: bfloat16 [2, 16384, 16384], P(None, ('groups', 'mp'), 'hidden'), parts along dimension 1, may hold values from -6 to 6
Outputs:
- outputs: bfloat16 [2048, 16384], P(('groups', 'mp'), 'hidden'), parts along dimension 0
- in_grad: bfloat16 [2048, 8192], P(('groups', 'hidden'), 'mp'), parts along dimension 0
- update: float32 [8192, 32768], P('mp', ('groups', 'hidden')), parts along dimension 1
The draws below stay inside these ranges and needn't reach their ends.
There are 2 independent parts, one for each index of `groups`. The reference program is written for one: setup_inputs(seed, part) draws one part's arguments, and reference() takes and returns one part's arrays. A program takes and returns all parts, laid end to end along the dimension named above; an argument that names none is the same for every part. Nothing has to cross between parts.
Inputs may be any that keep to these rules, and one draw needn't show every extreme that they name: `inputs`: Real-valued activations whose rows and columns carry independent scales. `out_grad`: Real-valued gradients whose rows and columns carry independent scales; examples differ in overall size.
All inputs are finite; a program needn't handle non-finite values.
Results may differ from the reference program's by a relative error of at most 0.0049.
Values may be sent and summed in bfloat16 or wider, within the bound.
No kernel may reach another device: no remote copies, remote signals or barrier semaphores. Data moves between devices by JAX's collectives and lax.ppermute only.
A program may use at most 256 MiB of HBM per device.

```python
import math
import jax
import jax.numpy as jnp
from jax import lax

D = 8192
FF = 16384
SEQ = 64
EXAMPLES = 16


def column_scales(key, columns):
    spot = jnp.arange(columns, dtype=jnp.float32) / max(columns - 1, 1)
    jitter = jax.random.uniform(key, (columns,), jnp.float32, 0.0, math.log(3.5))
    return jnp.exp(math.log(3.0) * spot + jitter) / 3.0


def base_field(key, shape):
    first_key = jax.random.fold_in(key, 0)
    return jax.random.normal(first_key, shape, jnp.float32)


def draw_inputs(key, part):
    first_key, second_key, third_key = jax.random.split(jax.random.fold_in(key, 11), 3)
    total = EXAMPLES * SEQ
    values = base_field(first_key, (total, D))
    row_scale = jnp.exp(jax.random.uniform(second_key, (total, 1), jnp.float32, math.log(0.3), math.log(3.0)))
    return (values * row_scale * column_scales(third_key, D)[None, :]).astype(jnp.bfloat16)


def draw_out_grad(key, part):
    first_key, second_key, third_key, fourth_key, fifth_key = jax.random.split(jax.random.fold_in(key, 23), 5)
    total = EXAMPLES * SEQ
    values = base_field(first_key, (total, FF))
    row_scale = jnp.exp(jax.random.uniform(second_key, (total, 1), jnp.float32, math.log(0.3), math.log(3.0)))
    ranking = jax.random.permutation(third_key, EXAMPLES).astype(jnp.float32)
    jitter = jax.random.uniform(fourth_key, (EXAMPLES,), jnp.float32, 0.0, 1.0)
    example_scale = jnp.power(10.0, -(ranking + jitter) / EXAMPLES)
    token_scale = jnp.repeat(example_scale, SEQ)[:, None]
    return (values * row_scale * token_scale * column_scales(fifth_key, FF)[None, :]).astype(jnp.bfloat16)


def block_levels(stream_key, dims, pieces, smallest, top_value):
    level, own = 1.0, jax.random.fold_in(stream_key, 6)
    for axis_at, shards_of in pieces:
        heights = jnp.exp(jax.random.uniform(jax.random.fold_in(own, axis_at), (shards_of,), jnp.float32, smallest / len(pieces), top_value / len(pieces)))
        level = level * jnp.repeat(heights, dims[axis_at] // shards_of).reshape([-1 if axis == axis_at else 1 for axis in range(len(dims))])
    return level


def bell_draw(stream_key, dims, width, most, shards=(), kind=jnp.bfloat16):
    array = jax.random.normal(stream_key, dims, jnp.float32) * width
    if len(shards) > 0:
        array = block_levels(stream_key, dims, shards, -0.22, 0.18) * array
    return jnp.clip(array, min=-most, max=most).astype(kind)


def setup_inputs(seed: int = 0, part: int = 0) -> dict:
    streams_of = jax.random.split(jax.random.key(seed), 5)
    part_keys = jax.random.split(jax.random.fold_in(streams_of[4], part), 5)
    inputs = draw_inputs(jax.random.fold_in(jax.random.fold_in(streams_of[4], part), 71), part)
    out_grad = draw_out_grad(jax.random.fold_in(jax.random.fold_in(streams_of[4], part), 71), part)
    weight = bell_draw(streams_of[2], (D, FF), D ** -0.5, 0.0625, ((0, 4), (1, 4)), jnp.float32)
    noise = bell_draw(part_keys[3], (2, D, FF), 1.0, 6.0, ((1, 4), (2, 4)))
    return {"inputs": inputs, "out_grad": out_grad, "weight": weight, "noise": noise}


def reference(inputs, out_grad, weight, noise):
    weight_half = weight.astype(jnp.bfloat16)
    outputs = jnp.dot(inputs, weight_half, preferred_element_type=jnp.float32).astype(jnp.bfloat16)
    in_grad = jnp.dot(out_grad, weight_half.T, preferred_element_type=jnp.float32).astype(jnp.bfloat16)
    feature_blocks = inputs.astype(jnp.float32).reshape(EXAMPLES, SEQ, D)
    unit_blocks = out_grad.astype(jnp.float32).reshape(EXAMPLES, SEQ, FF)
    feature_gram = jnp.einsum('bsd,btd->bst', feature_blocks, feature_blocks, precision=lax.Precision.HIGHEST)
    unit_gram = jnp.einsum('bsd,btd->bst', unit_blocks, unit_blocks, precision=lax.Precision.HIGHEST)
    squares = lax.optimization_barrier(jnp.sum(feature_gram * unit_gram, axis=(1, 2)))
    clip_norm = math.sqrt(SEQ * D * FF)
    factor = jnp.minimum(1.0, clip_norm / jnp.sqrt(squares + 1e-06))
    scaled_grad = (unit_blocks * factor[:, None, None]).reshape(EXAMPLES * SEQ, FF).astype(jnp.bfloat16)
    weight_grad = jnp.dot(inputs.T, scaled_grad, preferred_element_type=jnp.float32)
    band_noise = noise[0].astype(jnp.float32) - 0.6 * noise[1].astype(jnp.float32)
    update = (weight_grad * (math.sqrt(D * FF) / clip_norm) + 4.0 * band_noise) / EXAMPLES
    return (outputs, in_grad, update)
```

```python
import math

import jax
import jax.numpy as jnp
from jax import lax
from jax.experimental import pallas as pl
from jax.experimental.pallas import tpu as pltpu
from jax.sharding import PartitionSpec as P

SEQ = 64
NOISE_BAND = 0.6
NOISE_SCALE = 4.0
VMEM = 60 * 1024 * 1024
F32 = jnp.float32
BF16 = jnp.bfloat16
ANY = pl.BlockSpec(memory_space=pl.ANY)


def params(dims):
    return pltpu.CompilerParams(
        vmem_limit_bytes=VMEM, dimension_semantics=("arbitrary",) * dims
    )


def whole(shape):
    return pl.BlockSpec(shape, lambda *_: (0,) * len(shape))


def pair_kernel(transposed, place, finish, count, merged, extra, at, *refs):
    pieces, w = refs[:count], refs[count]
    merges = refs[count + 1 : count + 1 + merged]
    *products, full, rows = refs[count + 1 + merged + extra :]
    r = rows.shape[0] // 2

    @pl.when(pl.program_id(0) == 0)
    def _():
        for cond, slot, spot, piece in place(at, pieces):

            def put(slot=slot, spot=spot, piece=piece):
                rows[pl.ds(pl.multiple_of(slot * r, r), r), :] = piece[...]
                full[spot] = piece[...]

            if cond is None:
                put()
            else:
                pl.when(cond)(put)

    tile = w[...]
    if tile.dtype != BF16:
        tile = tile.astype(BF16)
        products[-1][...] = tile
    dims = (((1,), (1 if transposed else 0,)), ((), ()))
    total = lax.dot_general(rows[...], tile, dims, preferred_element_type=F32)
    finish(at, total[:r], total[r:], merges, products)


def pair_matmul(at, pair, pieces, w, place, transposed, finish, outs, merges, before, after, name):
    r, depth = pieces[0].shape
    width = w.shape[0] if transposed else w.shape[1]
    cast = w.dtype != BF16
    tile = min(256 if cast else 512 if transposed else 1024, width)
    w_spec = (
        pl.BlockSpec((tile, depth), lambda i, at: (i, 0))
        if transposed
        else pl.BlockSpec((depth, tile), lambda i, at: (0, i))
    )
    extra = ([] if before is None else [before]) + list(after)
    count = len(pieces)
    product = pl.BlockSpec((r, tile), lambda i, at: (0, i))
    kernel = lambda *refs: pair_kernel(
        transposed, place, finish, count, len(merges), len(extra), *refs
    )
    return pl.pallas_call(
        kernel,
        grid_spec=pltpu.PrefetchScalarGridSpec(
            num_scalar_prefetch=1,
            grid=(width // tile,),
            in_specs=[whole((r, depth))] * count
            + [w_spec]
            + [product] * len(merges)
            + [ANY] * len(extra),
            out_specs=[product] * outs
            + [w_spec] * cast
            + [pl.BlockSpec((2, r, depth), lambda i, at: (at[pair], 0, 0))],
            scratch_shapes=[pltpu.VMEM((2 * r, depth), BF16)],
        ),
        out_shape=[jax.ShapeDtypeStruct((r, width), BF16)] * outs
        + [jax.ShapeDtypeStruct(w.shape, BF16)] * cast
        + [jax.ShapeDtypeStruct((4, r, depth), BF16)],
        input_output_aliases={}
        if before is None
        else {count + 2 + len(merges): outs + cast},
        compiler_params=params(1),
        cost_estimate=pl.CostEstimate(
            flops=4 * r * depth * width,
            bytes_accessed=(6 if cast else 2) * depth * width + 4 * r * (width + depth),
            transcendentals=0,
        ),
        name=name,
    )(at, *pieces, w, *merges, *extra)


def update_kernel(gain, count, factor, x, g, noise, out, scaled):
    @pl.when(pl.program_id(0) == 0)
    def _():
        for t in range(0, scaled.shape[0], SEQ):
            span = pl.ds(t, SEQ)
            scaled[span, :] = (g[span, :].astype(F32) * factor[span, :]).astype(BF16)

    step = min(1024, out.shape[1])
    for j in range(0, out.shape[1], step):
        span = pl.ds(j, step)
        grad = lax.dot_general(
            x[...], scaled[:, span], (((0,), (0,)), ((), ())), preferred_element_type=F32
        )
        band = noise[0, :, span].astype(F32) - NOISE_BAND * noise[1, :, span].astype(F32)
        out[:, span] = (grad * gain + NOISE_SCALE * band) * (1.0 / count)


def make_update(x, g, factor, noise, gain, count, part=0, parts=1, before=None, after=()):
    tokens, depth = x.shape
    whole_width = g.shape[1]
    width = whole_width // parts
    tile = min(256, depth)
    extra = ([] if before is None else [before]) + list(after)

    def kernel(factor, x, g, noise, *refs):
        update_kernel(gain, count, factor, x, g, noise, *refs[len(extra) :])

    return pl.pallas_call(
        kernel,
        grid=(depth // tile,),
        in_specs=[
            whole((tokens, 1)),
            pl.BlockSpec((tokens, tile), lambda i: (0, i)),
            pl.BlockSpec((tokens, width), lambda i: (0, part)),
            pl.BlockSpec((2, tile, width), lambda i: (0, i, part)),
        ]
        + [ANY] * len(extra),
        out_specs=pl.BlockSpec((tile, width), lambda i: (i, part)),
        out_shape=jax.ShapeDtypeStruct((depth, whole_width), F32),
        scratch_shapes=[pltpu.VMEM((tokens, width), BF16)],
        input_output_aliases={} if before is None else {4: 0},
        compiler_params=params(1),
        cost_estimate=pl.CostEstimate(
            flops=2 * tokens * depth * width,
            bytes_accessed=(8 * depth * width + 2 * tokens * (depth + width)),
            transcendentals=0,
        ),
        name="update",
    )(factor, x, g, noise, *extra)


OUTER = [(0, 1), (1, 0), (2, 3), (3, 2)]
MIDDLE = [(1, 2), (2, 1)]
INWARD = [(0, 1), (3, 2)]
OUTWARD = [(1, 0), (2, 3)]


def along(value, pairs):
    return lax.ppermute(value, "hidden", pairs)


def swap(value, bit):
    return lax.ppermute(value, "mp", [(i, i ^ bit) for i in range(4)])


def gram(rows):
    blocks = rows.reshape(-1, SEQ, rows.shape[1])
    return jnp.einsum("bsd,btd->bst", blocks, blocks, preferred_element_type=F32)


def gram_pairs(rows):
    blocks = gram(rows).astype(BF16)
    return jnp.concatenate([blocks[0::2], blocks[1::2]], axis=2)


def factor_kernel(clip, pairs, at, f, u, got, out):
    h, m = at[4], at[5]
    blocks = 2 * u.shape[0] // (2 * pairs)
    r = out.shape[0] // blocks
    half = f.shape[0]
    lane = lax.broadcasted_iota(jnp.int32, (1, 2 * SEQ), 1)

    def sums(block):
        j, i = block ^ h, block ^ m
        for p in range(pairs):
            unit = u[i * pairs + p].astype(F32) + got[half + i * pairs + p].astype(F32)
            spot = j * pairs + p
            mine = f[jnp.minimum(spot, half - 1)].astype(F32)
            feature = jnp.where(spot < half, mine, got[jnp.maximum(spot - half, 0)].astype(F32))
            yield p, jnp.sum(feature * unit, axis=0, keepdims=True)

    for block in range(blocks):
        for p, total in sums(block):
            for side in range(2):
                square = jnp.sum(
                    jnp.where(lane // SEQ == side, total, 0.0), axis=1, keepdims=True
                )
                factor = jnp.minimum(1.0, clip / jnp.sqrt(square + 1e-06))
                start = block * r + (2 * p + side) * SEQ
                out[start : start + SEQ, :] = jnp.broadcast_to(factor, (SEQ, 1))


def make_factor(at, f, u, got, clip, pairs, tokens):
    return pl.pallas_call(
        lambda *refs: factor_kernel(clip, pairs, *refs),
        in_specs=[pl.BlockSpec(memory_space=pltpu.SMEM)]
        + [pl.BlockSpec(memory_space=pltpu.VMEM)] * 3,
        out_specs=pl.BlockSpec(memory_space=pltpu.VMEM),
        out_shape=jax.ShapeDtypeStruct((tokens, 1), F32),
        name="clip_factor",
    )(at, f, u, got)


def plus(a, b):
    return (a.astype(F32) + b.astype(F32)).astype(BF16)


def pipelined(inputs, out_grad, weight, noise):
    n = 4
    m, h = lax.axis_index("mp"), lax.axis_index("hidden")
    at = jnp.stack([h // 2, 1 - h // 2, m // 2, 1 - m // 2, h, m]).astype(jnp.int32)
    d_all, ff_all = inputs.shape[1] * n, out_grad.shape[1] * n
    tokens = inputs.shape[0] * n
    examples = inputs.shape[0] // SEQ
    clip = math.sqrt(SEQ * d_all * ff_all)

    hold = lax.optimization_barrier
    g_side = swap(out_grad, 1)
    g_far = swap(out_grad, 2)
    x_side = along(inputs, OUTER)
    x_mid = along(inputs, MIDDLE)
    features, units = gram_pairs(inputs), gram_pairs(out_grad)
    pairs = features.shape[0]
    grams = swap(jnp.concatenate([features, units]), 1)
    weight, g_side, features, units = hold((weight, g_side, features, units))

    def out_grad_rows(at, pieces):
        h, core, half = at[4], at[5] & 1, at[2]

        def slot(block_core, near):
            return jnp.where(near, (block_core ^ h ^ 1) & 1, block_core ^ at[4] // 2 ^ 1)

        near = half == at[0]
        return [
            (None, slot(core, near), core, pieces[0]),
            (None, slot(1 - core, near), 1 - core, pieces[1]),
        ]

    def far_out_grad_rows(at, pieces):
        h, core, half = at[4], at[5] & 1, at[3]
        near = half == at[0]

        def slot(block_core):
            return jnp.where(near, (block_core ^ h ^ 1) & 1, block_core ^ at[4] // 2 ^ 1)

        return [
            (None, slot(core), core, pieces[0]),
            (None, slot(1 - core), 1 - core, pieces[1]),
        ]

    def near_rows(at, pieces):
        odd, core = at[4] & 1, at[5] & 1
        return [
            (None, odd ^ core, odd, pieces[0]),
            (None, 1 - (odd ^ core), 1 - odd, pieces[1]),
        ]

    def far_rows(at, pieces):
        up, core = at[0], at[5] & 1
        inner = (at[4] == 1) | (at[4] == 2)
        outer = jnp.logical_not(inner)
        return [
            (inner, up ^ core, up, pieces[0]),
            (outer, up ^ core, up, pieces[1]),
            (inner, 1 - (up ^ core), 1 - up, pieces[2]),
            (outer, 1 - (up ^ core), 1 - up, pieces[3]),
        ]

    def plainly(at, first, second, merges, products):
        products[0][...] = first.astype(BF16)
        products[1][...] = second.astype(BF16)

    def in_grad_order(at, first, second, merges, products):
        near_last = at[2] == at[0]

        @pl.when(near_last)
        def _():
            products[0][...], products[1][...] = first.astype(BF16), second.astype(BF16)
            products[2][...], products[3][...] = merges[0][...], merges[1][...]

        @pl.when(jnp.logical_not(near_last))
        def _():
            products[0][...], products[1][...] = merges[0][...], merges[1][...]
            products[2][...], products[3][...] = first.astype(BF16), second.astype(BF16)

    def outputs_order(at, first, second, merges, products):
        near = (merges[0][...].astype(F32) + merges[1][...].astype(F32)).astype(BF16)
        near_mine = at[2] == at[0]
        products[2][...] = second.astype(BF16)

        @pl.when(near_mine)
        def _():
            products[0][...], products[1][...] = first.astype(BF16), near

        @pl.when(jnp.logical_not(near_mine))
        def _():
            products[0][...], products[1][...] = near, first.astype(BF16)

    qa0, qa1, w, g_half = pair_matmul(
        at, 2, [out_grad, g_side], weight, out_grad_rows, True, plainly, 2, [], None, [], "in_grad_here"
    )
    x_side, x_mid, w, grams = hold((x_side, x_mid, w, grams))
    features = plus(features, grams[:pairs])
    units = jnp.concatenate([units, grams[pairs:]])
    grams = swap(jnp.concatenate([features, units]), 2)
    x_mid2 = along(x_side, MIDDLE)
    x_out = along(x_mid, OUTWARD)
    pa0, pa1, x_half = pair_matmul(
        at, 0, [inputs, x_side], w, near_rows, False, plainly, 2, [], None, [], "outputs_near"
    )
    g_far, pa1, x_mid2, x_out, grams = hold((g_far, pa1, x_mid2, x_out, grams))
    g_far_side = swap(g_far, 1)
    x_out2 = along(x_mid2, OUTWARD)
    pa1 = swap(pa1, 1)
    features = plus(features, grams[:pairs])
    units = jnp.concatenate([units, grams[pairs:]])
    grams = along(jnp.concatenate([features, units]), OUTER)
    first, second, beside, own, g_all = pair_matmul(
        at, 3, [g_far, g_far_side], w, far_out_grad_rows, True, in_grad_order, 4, [qa0, qa1], g_half, [pa0], "in_grad_there"
    )
    grams, first, x_out2 = hold((grams, first, x_out2))
    r1a = along(first, INWARD)
    features = jnp.concatenate([features, grams[:pairs]])
    units = plus(units, grams[pairs:])
    grams = along(jnp.concatenate([features, units]), [(i, i ^ 2) for i in range(n)])
    other, mine, pb1, x_all = pair_matmul(
        at, 1, [x_mid, x_out, x_mid2, x_out2], w, far_rows, False, outputs_order, 3, [pa0, pa1], x_half, [first], "outputs_far"
    )
    same = m // 2 == h // 2
    r1a, pb1 = hold((r1a, pb1))
    pb1 = swap(pb1, 1)
    r2a = along(plus(first, r1a), MIDDLE)
    r1b = along(second, INWARD)
    other = plus(other, jnp.where(same, pb1, 0))
    theirs = swap(other, 2)

    grams, other = hold((grams, other))
    factor = make_factor(at, features, units, grams, clip, pairs, tokens)
    x_all, g_all = x_all.reshape(tokens, -1), g_all.reshape(tokens, -1)
    gain = math.sqrt(d_all * ff_all) / clip
    update = make_update(x_all, g_all, factor, noise, gain, tokens // SEQ, 0, 2, None, [other])
    r2a, r1b, update = hold((r2a, r1b, update))
    r3 = along(plus(beside, r2a), OUTER)
    r2b = along(plus(second, r1b), MIDDLE)
    update = make_update(x_all, g_all, factor, noise, gain, tokens // SEQ, 1, 2, update)
    r3, r2b, theirs, update = hold((r3, r2b, theirs, update))
    in_grad = (own.astype(F32) + r3.astype(F32) + r2b.astype(F32)).astype(BF16)
    mine = mine.astype(F32) + jnp.where(same, 0, pb1).astype(F32)
    outputs = (mine + theirs.astype(F32)).astype(BF16)
    return outputs, in_grad, update


def plain(tokens, d_all, ff_all, inputs, out_grad, weight, noise):
    w = weight.astype(BF16)
    x = lax.all_gather(inputs, "hidden", axis=0, tiled=True)
    g = lax.all_gather(out_grad, "mp", axis=0, tiled=True)
    clip = math.sqrt(SEQ * d_all * ff_all)
    outputs = lax.psum_scatter(
        jnp.dot(x, w, preferred_element_type=F32), "mp", scatter_dimension=0, tiled=True
    )
    in_grad = lax.psum_scatter(
        lax.dot_general(g, w, (((1,), (1,)), ((), ())), preferred_element_type=F32),
        "hidden",
        scatter_dimension=0,
        tiled=True,
    )
    grams = lax.psum(gram(x), "mp") * lax.psum(gram(g), "hidden")
    factor = jnp.minimum(1.0, clip / jnp.sqrt(jnp.sum(grams, axis=(1, 2)) + 1e-06))
    update = make_update(
        x,
        g,
        jnp.repeat(factor, SEQ)[:, None],
        noise,
        math.sqrt(d_all * ff_all) / clip,
        tokens // SEQ,
    )
    return outputs.astype(BF16), in_grad.astype(BF16), update


def solution(mesh):
    mp, hidden = mesh.shape["mp"], mesh.shape["hidden"]

    def shards(inputs, out_grad, weight, noise):
        if mp == hidden == 4 and inputs.shape[0] % (2 * SEQ) == 0:
            return pipelined(inputs, out_grad, weight, noise)
        return plain(
            inputs.shape[0] * hidden,
            inputs.shape[1] * mp,
            out_grad.shape[1] * hidden,
            inputs,
            out_grad,
            weight,
            noise,
        )

    in_specs = (
        P(("groups", "hidden"), "mp"),
        P(("groups", "mp"), "hidden"),
        P("mp", "hidden"),
        P(None, ("groups", "mp"), "hidden"),
    )
    out_specs = (
        P(("groups", "mp"), "hidden"),
        P(("groups", "hidden"), "mp"),
        P("mp", ("groups", "hidden")),
    )
    return jax.shard_map(shards, mesh=mesh, in_specs=in_specs, out_specs=out_specs, check_vma=False)
```

```python
import math

import jax
import jax.numpy as jnp
from jax import lax
from jax.experimental import pallas as pl
from jax.experimental.pallas import tpu as pltpu
from jax.sharding import PartitionSpec as P

SEQ = 64
NOISE_BAND = 0.6
NOISE_SCALE = 4.0
VMEM = 60 * 1024 * 1024
F32 = jnp.float32
BF16 = jnp.bfloat16
ANY = pl.BlockSpec(memory_space=pl.ANY)
BRIEF = pl.CostEstimate(flops=1, bytes_accessed=1, transcendentals=0)


def params(dims):
    return pltpu.CompilerParams(
        vmem_limit_bytes=VMEM, dimension_semantics=("arbitrary",) * dims
    )


def whole(shape):
    return pl.BlockSpec(shape, lambda *_: (0,) * len(shape))


def pair_kernel(transposed, place, finish, count, merged, extra, keep, at, *refs):
    pieces, w = refs[:count], refs[count]
    merges = refs[count + 1 : count + 1 + merged]
    *products, rows = refs[count + 1 + merged + extra :]
    kept = products.pop() if keep else None
    r = rows.shape[0] // 2

    @pl.when(pl.program_id(0) == 0)
    def _():
        for cond, slot, spot, piece in place(at, pieces):

            def put(slot=slot, spot=spot, piece=piece):
                rows[pl.ds(pl.multiple_of(slot * r, r), r), :] = piece[...]
                if keep:
                    kept[spot] = piece[...]

            if cond is None:
                put()
            else:
                pl.when(cond)(put)

    tile = w[...]
    if tile.dtype != BF16:
        tile = tile.astype(BF16)
        products[-1][...] = tile
    dims = (((1,), (1 if transposed else 0,)), ((), ()))
    total = lax.dot_general(rows[...], tile, dims, preferred_element_type=F32)
    finish(at, total[:r], total[r:], merges, products)


def pair_matmul(
    at, pieces, w, place, transposed, finish, outs, merges, after, name, keep=False, share=(0, 8), before=()
):
    r, depth = pieces[0].shape
    width = w.shape[0] if transposed else w.shape[1]
    cast = w.dtype != BF16
    tile = min(256 if cast else 512 if transposed else 1024, width)
    skip = width // tile * share[0] // 8
    steps = width // tile * share[1] // 8 - skip
    w_spec = (
        pl.BlockSpec((tile, depth), lambda i: (i + skip, 0))
        if transposed
        else pl.BlockSpec((depth, tile), lambda i: (0, i + skip))
    )
    extra = [*before, *after]
    count = len(pieces)
    first_extra = count + 2 + len(merges)
    product = pl.BlockSpec((r, tile), lambda i: (0, i + skip))
    kernel = lambda *refs: pair_kernel(
        transposed, place, finish, count, len(merges), len(extra), keep, *refs
    )
    return pl.pallas_call(
        kernel,
        grid=(steps,),
        in_specs=[pl.BlockSpec(memory_space=pltpu.SMEM)]
        + [whole((r, depth))] * count
        + [w_spec]
        + [product] * len(merges)
        + [ANY] * len(extra),
        out_specs=[product] * outs + [w_spec] * cast + [whole((2, r, depth))] * keep,
        scratch_shapes=[pltpu.VMEM((2 * r, depth), BF16)],
        out_shape=[jax.ShapeDtypeStruct((r, width), BF16)] * outs
        + [jax.ShapeDtypeStruct(w.shape, BF16)] * cast
        + [jax.ShapeDtypeStruct((2, r, depth), BF16)] * keep,
        input_output_aliases={first_extra + i: i for i in range(len(before))},
        compiler_params=params(1),
        cost_estimate=BRIEF,
        name=name,
    )(at, *pieces, w, *merges, *extra)


def update_kernel(gain, count, nx, ng, extra, slot_of, block_of, at, factor, *refs):
    xs, gs, noise = refs[:nx], refs[nx : nx + ng], refs[nx + ng]
    out, scaled, rows = refs[nx + ng + 1 + extra :]
    rx, rg = rows.shape[0] // nx, scaled.shape[0] // ng

    @pl.when(pl.program_id(0) == 0)
    def _():
        for j, g in enumerate(gs):
            block = block_of(at, j)
            source, target = block * rg, slot_of(at, block) * rg
            for t in range(0, rg, SEQ):
                scale = factor[pl.ds(pl.multiple_of(source + t, SEQ), SEQ), :]
                scaled[pl.ds(pl.multiple_of(target + t, SEQ), SEQ), :] = (
                    g[t : t + SEQ, :].astype(F32) * scale
                ).astype(BF16)

    for j, x in enumerate(xs):
        rows[j * rx : (j + 1) * rx, :] = x[...].reshape(rx, -1)
    step = min(1024, out.shape[1])
    for j in range(0, out.shape[1], step):
        span = pl.ds(j, step)
        grad = lax.dot_general(
            rows[...], scaled[:, span], (((0,), (0,)), ((), ())), preferred_element_type=F32
        )
        band = noise[0, :, span].astype(F32) - NOISE_BAND * noise[1, :, span].astype(F32)
        out[:, span] = (grad * gain + NOISE_SCALE * band) * (1.0 / count)


def make_update(
    at, xs, gs, slot_of, block_of, factor, noise, gain, count, part=0, parts=1, before=None, after=()
):
    tokens = factor.shape[0]
    depth, whole_width = noise.shape[1:]
    width = whole_width // parts
    tile = min(512, depth)
    rx, rg = tokens // len(xs), tokens // len(gs)
    extra = ([] if before is None else [before]) + list(after)

    def x_spec(lead):
        if lead is None:
            return pl.BlockSpec((rx, tile), lambda i: (0, i))
        return pl.BlockSpec((1, rx, tile), lambda i: (lead, 0, i))

    def kernel(*refs):
        update_kernel(gain, count, len(xs), len(gs), len(extra), slot_of, block_of, *refs)

    return pl.pallas_call(
        kernel,
        grid=(depth // tile,),
        in_specs=[pl.BlockSpec(memory_space=pltpu.SMEM), whole((tokens, 1))]
        + [x_spec(lead) for _, lead in xs]
        + [pl.BlockSpec((rg, width), lambda i: (0, part))] * len(gs)
        + [pl.BlockSpec((2, tile, width), lambda i: (0, i, part))]
        + [ANY] * len(extra),
        out_specs=pl.BlockSpec((tile, width), lambda i: (i, part)),
        out_shape=jax.ShapeDtypeStruct((depth, whole_width), F32),
        scratch_shapes=[pltpu.VMEM((tokens, width), BF16), pltpu.VMEM((tokens, tile), BF16)],
        input_output_aliases={} if before is None else {3 + len(xs) + len(gs): 0},
        compiler_params=params(1),
        cost_estimate=BRIEF,
        name="update",
    )(at, factor, *[x for x, _ in xs], *gs, noise, *extra)


def add_kernel(sums, ins, at, *refs):
    sums(at, refs[:ins], refs[ins:])


def add_up(at, sums, arrays, outs, steps, name):
    def band(shape):
        return pl.BlockSpec((shape[0] // steps, shape[1]), lambda i: (i, 0))

    return pl.pallas_call(
        lambda *refs: add_kernel(sums, len(arrays), *refs),
        grid=(steps,),
        in_specs=[pl.BlockSpec(memory_space=pltpu.SMEM)] + [band(x.shape) for x in arrays],
        out_specs=[band(shape) for shape in outs],
        out_shape=[jax.ShapeDtypeStruct(shape, BF16) for shape in outs],
        compiler_params=params(1),
        cost_estimate=BRIEF,
        name=name,
    )(at, *arrays)


def total(*refs):
    return sum(ref[...].astype(F32) for ref in refs)


OUTER = [(0, 1), (1, 0), (2, 3), (3, 2)]
MIDDLE = [(1, 2), (2, 1)]
INWARD = [(0, 1), (3, 2)]
OUTWARD = [(1, 0), (2, 3)]


def along(value, pairs):
    return lax.ppermute(value, "hidden", pairs)


def swap(value, bit):
    return lax.ppermute(value, "mp", [(i, i ^ bit) for i in range(4)])


def gram(rows):
    blocks = rows.reshape(-1, SEQ, rows.shape[1])
    return jnp.einsum("bsd,btd->bst", blocks, blocks, preferred_element_type=F32)


def gram_pairs(rows):
    blocks = gram(rows).astype(BF16)
    return jnp.concatenate([blocks[0::2], blocks[1::2]], axis=2)


def factor_kernel(clip, pairs, n, at, *refs):
    *grams, out = refs
    h, m = at[2], at[3]
    r = out.shape[0] // n
    lane = lax.broadcasted_iota(jnp.int32, (1, 2 * SEQ), 1)
    for i, gram in enumerate(grams):
        block = m ^ i
        for p in range(pairs):
            spot = (block ^ h) * pairs + p
            feature = sum(g[spot].astype(F32) for g in grams)
            products = feature * gram[n * pairs + p].astype(F32)
            sums = jnp.sum(products, axis=0, keepdims=True)
            for side in range(2):
                square = jnp.sum(
                    jnp.where(lane // SEQ == side, sums, 0.0), axis=1, keepdims=True
                )
                factor = jnp.minimum(1.0, clip / jnp.sqrt(square + 1e-06))
                start = pl.multiple_of(block * r + (2 * p + side) * SEQ, SEQ)
                out[pl.ds(start, SEQ), :] = jnp.broadcast_to(factor, (SEQ, 1))


def make_factor(at, grams, clip, pairs, tokens):
    return pl.pallas_call(
        lambda *refs: factor_kernel(clip, pairs, len(grams), *refs),
        in_specs=[pl.BlockSpec(memory_space=pltpu.SMEM)]
        + [pl.BlockSpec(memory_space=pltpu.VMEM)] * len(grams),
        out_specs=pl.BlockSpec(memory_space=pltpu.VMEM),
        out_shape=jax.ShapeDtypeStruct((tokens, 1), F32),
        cost_estimate=BRIEF,
        name="clip_factor",
    )(at, *grams)


def plus(a, b):
    return (a.astype(F32) + b.astype(F32)).astype(BF16)


def pipelined(inputs, out_grad, weight, noise):
    n = 4
    m, h = lax.axis_index("mp"), lax.axis_index("hidden")
    at = jnp.stack([h // 2, m // 2, h, m]).astype(jnp.int32)
    d_all, ff_all = inputs.shape[1] * n, out_grad.shape[1] * n
    tokens = inputs.shape[0] * n
    clip = math.sqrt(SEQ * d_all * ff_all)
    hold = lax.optimization_barrier

    g_side = swap(out_grad, 1)
    g_far = swap(out_grad, 2)
    x_side = along(inputs, OUTER)
    x_mid = along(inputs, MIDDLE)
    features, units = gram_pairs(inputs), gram_pairs(out_grad)
    pairs = features.shape[0]
    grams = along(jnp.concatenate([features, units]), OUTER)
    weight, g_side, features, units = hold((weight, g_side, features, units))


    def out_grad_rows(half):
        def place(at, pieces):
            core, near = at[3] & 1, half(at) == at[0]

            def slot(block_core):
                return jnp.where(near, (block_core ^ at[2] ^ 1) & 1, block_core ^ at[0] ^ 1)

            return [(None, slot(core), 0, pieces[0]), (None, slot(1 - core), 0, pieces[1])]

        return place

    def near_rows(at, pieces):
        slot = (at[2] ^ at[3]) & 1
        return [(None, slot, 0, pieces[0]), (None, 1 - slot, 0, pieces[1])]

    def far_rows(at, pieces):
        slot = (at[0] ^ at[3]) & 1
        inner = (at[2] == 1) | (at[2] == 2)
        outer = jnp.logical_not(inner)
        return [
            (inner, slot, 0, pieces[0]),
            (outer, slot, 0, pieces[1]),
            (inner, 1 - slot, 1, pieces[2]),
            (outer, 1 - slot, 1, pieces[3]),
        ]

    def plainly(at, first, second, merges, products):
        products[0][...] = first.astype(BF16)
        products[1][...] = second.astype(BF16)

    def in_grad_order(at, first, second, merges, products):
        near_first = at[0] == at[1]

        @pl.when(near_first)
        def _():
            products[0][...], products[1][...] = first.astype(BF16), second.astype(BF16)
            products[2][...], products[3][...] = merges[0][...], merges[1][...]

        @pl.when(jnp.logical_not(near_first))
        def _():
            products[0][...], products[1][...] = merges[0][...], merges[1][...]
            products[2][...], products[3][...] = first.astype(BF16), second.astype(BF16)

    def outputs_order(at, first, second, merges, products):
        near = total(*merges).astype(BF16)
        near_mine = at[0] == at[1]
        products[2][...] = second.astype(BF16)

        @pl.when(near_mine)
        def _():
            products[0][...], products[1][...] = first.astype(BF16), near

        @pl.when(jnp.logical_not(near_mine))
        def _():
            products[0][...], products[1][...] = near, first.astype(BF16)

    def rows_here(share, before):
        return pair_matmul(
            at, [out_grad, g_side], weight, out_grad_rows(lambda at: at[1]), True, plainly, 2, [], [units],
            "in_grad_here", share=share, before=before,
        )

    x_side, x_mid, grams, *qa = hold((x_side, x_mid, grams, *rows_here((0, 5), ())))
    x_mid2 = along(x_side, MIDDLE)
    x_out = along(x_mid, OUTWARD)
    qa0, qa1, w = rows_here((5, 8), qa)
    pa0, pa1 = pair_matmul(
        at, [inputs, x_side], w, near_rows, False, plainly, 2, [], [], "outputs_near"
    )
    g_far, pa1, x_mid2, x_out, grams = hold((g_far, pa1, x_mid2, x_out, grams))
    features = jnp.concatenate([features, grams[:pairs]])
    units = plus(units, grams[pairs:])
    grams = along(jnp.concatenate([features, units]), [(i, i ^ 2) for i in range(n)])
    g_far_side = swap(g_far, 1)
    x_out2 = along(x_mid2, OUTWARD)
    pa1 = swap(pa1, 1)
    first, second, beside, own = pair_matmul(
        at, [g_far, g_far_side], w, out_grad_rows(lambda at: 1 - at[1]), True, in_grad_order, 4,
        [qa0, qa1], [pa0], "in_grad_there",
    )
    grams, first = hold((grams, first))
    grams = jnp.concatenate(
        [features, grams[: 2 * pairs], plus(units, grams[2 * pairs :])]
    )
    others = [swap(grams, j) for j in range(1, n)]
    r1a = along(first, INWARD)
    other, mine, pb1, x_far = pair_matmul(
        at, [x_mid, x_out, x_mid2, x_out2], w, far_rows, False, outputs_order, 3,
        [pa0, pa1], [first], "outputs_far", keep=True,
    )
    r1a, pb1, others = hold((r1a, pb1, others))
    pb1 = swap(pb1, 1)

    def now(at, refs, outs):
        outs[0][...] = total(refs[0], refs[1]).astype(BF16)
        side = jnp.where(at[0] == at[1], refs[3][...].astype(F32), 0.0)
        outs[1][...] = (refs[2][...].astype(F32) + side).astype(BF16)

    def later(at, refs, outs):
        outs[0][...] = total(refs[0], refs[1]).astype(BF16)
        outs[1][...] = total(refs[2], refs[3]).astype(BF16)

    def last(at, refs, outs):
        outs[0][...] = total(refs[0], refs[1], refs[2]).astype(BF16)
        side = jnp.where(at[0] == at[1], 0.0, refs[4][...].astype(F32))
        outs[1][...] = (total(refs[3], refs[5]) + side).astype(BF16)

    narrow, wide = first.shape, other.shape
    r2a, other = add_up(at, now, [first, r1a, other, pb1], [narrow, wide], 2, "sums_now")
    r2a = along(r2a, MIDDLE)
    r1b = along(second, INWARD)
    theirs = swap(other, 2)
    factor = make_factor(at, [grams, *others], clip, pairs, tokens)

    def block_of(at, j):
        return at[3] ^ j

    def slot_of(at, block):
        far = jnp.where(at[0] == 0, block, 3 - block)
        return jnp.where(block // 2 == at[0], (block ^ at[2]) & 1, far)

    xs = [(inputs, None), (x_side, None), (x_far, 0), (x_far, 1)]
    gs = [out_grad, g_side, g_far, g_far_side]
    gain = math.sqrt(d_all * ff_all) / clip
    facts = (slot_of, block_of, factor, noise, gain, tokens // SEQ)
    update = make_update(at, xs, gs, *facts, 0, 2, None, [other])
    r2a, r1b, update = hold((r2a, r1b, update))
    r3, r2b = add_up(at, later, [beside, r2a, second, r1b], [narrow, narrow], 2, "sums_later")
    r3 = along(r3, OUTER)
    r2b = along(r2b, MIDDLE)
    update = make_update(at, xs, gs, *facts, 1, 2, update)
    r3, r2b, theirs, update = hold((r3, r2b, theirs, update))
    in_grad, outputs = add_up(
        at, last, [own, r3, r2b, mine, pb1, theirs], [narrow, wide], 4, "sums_last"
    )
    return outputs, in_grad, update


def plain(tokens, d_all, ff_all, inputs, out_grad, weight, noise):
    w = weight.astype(BF16)
    x = lax.all_gather(inputs, "hidden", axis=0, tiled=True)
    g = lax.all_gather(out_grad, "mp", axis=0, tiled=True)
    clip = math.sqrt(SEQ * d_all * ff_all)
    outputs = lax.psum_scatter(
        jnp.dot(x, w, preferred_element_type=F32), "mp", scatter_dimension=0, tiled=True
    )
    in_grad = lax.psum_scatter(
        lax.dot_general(g, w, (((1,), (1,)), ((), ())), preferred_element_type=F32),
        "hidden",
        scatter_dimension=0,
        tiled=True,
    )
    grams = lax.psum(gram(x), "mp") * lax.psum(gram(g), "hidden")
    factor = jnp.minimum(1.0, clip / jnp.sqrt(jnp.sum(grams, axis=(1, 2)) + 1e-06))
    none = lambda at, j: 0
    update = make_update(
        jnp.zeros((1,), jnp.int32),
        [(x, None)],
        [g],
        none,
        none,
        jnp.repeat(factor, SEQ)[:, None],
        noise,
        math.sqrt(d_all * ff_all) / clip,
        tokens // SEQ,
    )
    return outputs.astype(BF16), in_grad.astype(BF16), update


def solution(mesh):
    mp, hidden = mesh.shape["mp"], mesh.shape["hidden"]

    def shards(inputs, out_grad, weight, noise):
        if mp == hidden == 4 and inputs.shape[0] % (2 * SEQ) == 0:
            return pipelined(inputs, out_grad, weight, noise)
        return plain(
            inputs.shape[0] * hidden,
            inputs.shape[1] * mp,
            out_grad.shape[1] * hidden,
            inputs,
            out_grad,
            weight,
            noise,
        )

    in_specs = (
        P(("groups", "hidden"), "mp"),
        P(("groups", "mp"), "hidden"),
        P("mp", "hidden"),
        P(None, ("groups", "mp"), "hidden"),
    )
    out_specs = (
        P(("groups", "mp"), "hidden"),
        P(("groups", "hidden"), "mp"),
        P("mp", ("groups", "hidden")),
    )
    return jax.shard_map(shards, mesh=mesh, in_specs=in_specs, out_specs=out_specs, check_vma=False)
```

```python
import math

import jax
import jax.numpy as jnp
from jax import lax
from jax.experimental import pallas as pl
from jax.experimental.pallas import tpu as pltpu
from jax.sharding import PartitionSpec as P

SEQ = 64
NOISE_BAND = 0.6
NOISE_SCALE = 4.0
VMEM = 63 * 1024 * 1024
F32 = jnp.float32
BF16 = jnp.bfloat16
ANY = pl.BlockSpec(memory_space=pl.ANY)
BRIEF = pl.CostEstimate(flops=1, bytes_accessed=1, transcendentals=0)


def params(dims):
    return pltpu.CompilerParams(
        vmem_limit_bytes=VMEM, dimension_semantics=("arbitrary",) * dims
    )


def whole(shape):
    return pl.BlockSpec(shape, lambda *_: (0,) * len(shape))


def pair_kernel(transposed, place, finish, count, merged, extra, keep, at, *refs):
    pieces, w = refs[:count], refs[count]
    merges = refs[count + 1 : count + 1 + merged]
    *products, rows = refs[count + 1 + merged + extra :]
    kept = products.pop() if keep else None
    r = rows.shape[0] // 2

    @pl.when(pl.program_id(0) == 0)
    def _():
        for cond, slot, spot, piece in place(at, pieces):

            def put(slot=slot, spot=spot, piece=piece):
                rows[pl.ds(pl.multiple_of(slot * r, r), r), :] = piece[...]
                if keep:
                    kept[spot] = piece[...]

            if cond is None:
                put()
            else:
                pl.when(cond)(put)

    tile = w[...]
    if tile.dtype != BF16:
        tile = tile.astype(BF16)
        products[-1][...] = tile
    dims = (((1,), (1 if transposed else 0,)), ((), ()))
    total = lax.dot_general(rows[...], tile, dims, preferred_element_type=F32)
    finish(at, total[:r], total[r:], merges, products)


def pair_matmul(
    at, pieces, w, place, transposed, finish, outs, merges, after, name, keep=False, share=(0, 8), before=()
):
    r, depth = pieces[0].shape
    width = w.shape[0] if transposed else w.shape[1]
    cast = w.dtype != BF16
    tile = min(256 if cast else 512 if transposed else 1024, width)
    skip = width // tile * share[0] // 8
    steps = width // tile * share[1] // 8 - skip
    w_spec = (
        pl.BlockSpec((tile, depth), lambda i: (i + skip, 0))
        if transposed
        else pl.BlockSpec((depth, tile), lambda i: (0, i + skip))
    )
    extra = [*before, *after]
    count = len(pieces)
    first_extra = count + 2 + len(merges)
    product = pl.BlockSpec((r, tile), lambda i: (0, i + skip))
    kernel = lambda *refs: pair_kernel(
        transposed, place, finish, count, len(merges), len(extra), keep, *refs
    )
    return pl.pallas_call(
        kernel,
        grid=(steps,),
        in_specs=[pl.BlockSpec(memory_space=pltpu.SMEM)]
        + [whole((r, depth))] * count
        + [w_spec]
        + [product] * len(merges)
        + [ANY] * len(extra),
        out_specs=[product] * outs + [w_spec] * cast + [whole((2, r, depth))] * keep,
        scratch_shapes=[pltpu.VMEM((2 * r, depth), BF16)],
        out_shape=[jax.ShapeDtypeStruct((r, width), BF16)] * outs
        + [jax.ShapeDtypeStruct(w.shape, BF16)] * cast
        + [jax.ShapeDtypeStruct((2, r, depth), BF16)] * keep,
        input_output_aliases={first_extra + i: i for i in range(len(before))},
        compiler_params=params(1),
        cost_estimate=BRIEF,
        name=name,
    )(at, *pieces, w, *merges, *extra)


def update_kernel(gain, count, nx, ng, extra, slot_of, block_of, at, factor, *refs):
    xs, gs, noise = refs[:nx], refs[nx : nx + ng], refs[nx + ng]
    out, scaled, rows = refs[nx + ng + 1 + extra :]
    rx, rg = rows.shape[0] // nx, scaled.shape[0] // ng

    @pl.when(pl.program_id(0) == 0)
    def _():
        for j, g in enumerate(gs):
            block = block_of(at, j)
            source, target = block * rg, slot_of(at, block) * rg
            for t in range(0, rg, SEQ):
                scale = factor[pl.ds(pl.multiple_of(source + t, SEQ), SEQ), :]
                scaled[pl.ds(pl.multiple_of(target + t, SEQ), SEQ), :] = (
                    g[t : t + SEQ, :].astype(F32) * scale
                ).astype(BF16)

    for j, x in enumerate(xs):
        rows[j * rx : (j + 1) * rx, :] = x[...].reshape(rx, -1)
    step = min(1024, out.shape[1])
    for j in range(0, out.shape[1], step):
        span = pl.ds(j, step)
        grad = lax.dot_general(
            rows[...], scaled[:, span], (((0,), (0,)), ((), ())), preferred_element_type=F32
        )
        band = noise[0, :, span].astype(F32) - NOISE_BAND * noise[1, :, span].astype(F32)
        out[:, span] = (grad * gain + NOISE_SCALE * band) * (1.0 / count)


def make_update(
    at, xs, gs, slot_of, block_of, factor, noise, gain, count, part=0, parts=1, before=None, after=()
):
    tokens = factor.shape[0]
    depth, whole_width = noise.shape[1:]
    width = whole_width // parts
    tile = min(512, depth)
    rx, rg = tokens // len(xs), tokens // len(gs)
    extra = ([] if before is None else [before]) + list(after)

    def x_spec(lead):
        if lead is None:
            return pl.BlockSpec((rx, tile), lambda i: (0, i))
        return pl.BlockSpec((1, rx, tile), lambda i: (lead, 0, i))

    def kernel(*refs):
        update_kernel(gain, count, len(xs), len(gs), len(extra), slot_of, block_of, *refs)

    return pl.pallas_call(
        kernel,
        grid=(depth // tile,),
        in_specs=[pl.BlockSpec(memory_space=pltpu.SMEM), whole((tokens, 1))]
        + [x_spec(lead) for _, lead in xs]
        + [pl.BlockSpec((rg, width), lambda i: (0, part))] * len(gs)
        + [pl.BlockSpec((2, tile, width), lambda i: (0, i, part))]
        + [ANY] * len(extra),
        out_specs=pl.BlockSpec((tile, width), lambda i: (i, part)),
        out_shape=jax.ShapeDtypeStruct((depth, whole_width), F32),
        scratch_shapes=[pltpu.VMEM((tokens, width), BF16), pltpu.VMEM((tokens, tile), BF16)],
        input_output_aliases={} if before is None else {3 + len(xs) + len(gs): 0},
        compiler_params=params(1),
        cost_estimate=BRIEF,
        name="update",
    )(at, factor, *[x for x, _ in xs], *gs, noise, *extra)


def add_kernel(sums, ins, at, *refs):
    sums(at, refs[:ins], refs[ins:])


def add_up(at, sums, arrays, choices, outs, steps, name):
    def band(shape, cond=None):
        def index(i, at):
            return (i if cond is None else jnp.where(cond(at), i, 0), 0)

        return pl.BlockSpec((shape[0] // steps, shape[1]), index)

    arrays, chosen = list(arrays), [x for _, x in choices]
    return pl.pallas_call(
        lambda *refs: add_kernel(sums, len(arrays) + len(chosen), *refs),
        grid_spec=pltpu.PrefetchScalarGridSpec(
            num_scalar_prefetch=1,
            grid=(steps,),
            in_specs=[band(x.shape) for x in arrays] + [band(x.shape, c) for c, x in choices],
            out_specs=[band(shape) for shape in outs],
        ),
        out_shape=[jax.ShapeDtypeStruct(shape, BF16) for shape in outs],
        compiler_params=params(1),
        cost_estimate=BRIEF,
        name=name,
    )(at, *arrays, *chosen)


def total(*refs):
    return sum(ref[...].astype(F32) for ref in refs)


OUTER = [(0, 1), (1, 0), (2, 3), (3, 2)]
OUTWARD = [(1, 0), (2, 3)]


def along(value, pairs):
    return lax.ppermute(value, "hidden", pairs)


def middle(value):
    pairs = [
        (m * 4 + h, m * 4 + 3 - h if h in (1, 2) else (m ^ 1) * 4 + h)
        for m in range(4)
        for h in range(4)
    ]
    return lax.ppermute(value, ("mp", "hidden"), pairs)


def swap(value, bit):
    return lax.ppermute(value, "mp", [(i, i ^ bit) for i in range(4)])


def gram(rows):
    blocks = rows.reshape(-1, SEQ, rows.shape[1])
    return jnp.einsum("bsd,btd->bst", blocks, blocks, preferred_element_type=F32)


def gram_pairs(rows):
    blocks = gram(rows).astype(BF16)
    return jnp.concatenate([blocks[0::2], blocks[1::2]], axis=2)


def factor_kernel(clip, pairs, n, at, *refs):
    *grams, out = refs
    h, m = at[2], at[3]
    r = out.shape[0] // n
    lane = lax.broadcasted_iota(jnp.int32, (1, 2 * SEQ), 1)
    for i, gram in enumerate(grams):
        block = m ^ i
        for p in range(pairs):
            spot = (block ^ h) * pairs + p
            feature = sum(g[spot].astype(F32) for g in grams)
            products = feature * gram[n * pairs + p].astype(F32)
            sums = jnp.sum(products, axis=0, keepdims=True)
            for side in range(2):
                square = jnp.sum(
                    jnp.where(lane // SEQ == side, sums, 0.0), axis=1, keepdims=True
                )
                factor = jnp.minimum(1.0, clip / jnp.sqrt(square + 1e-06))
                start = pl.multiple_of(block * r + (2 * p + side) * SEQ, SEQ)
                out[pl.ds(start, SEQ), :] = jnp.broadcast_to(factor, (SEQ, 1))


def make_factor(at, grams, clip, pairs, tokens):
    return pl.pallas_call(
        lambda *refs: factor_kernel(clip, pairs, len(grams), *refs),
        in_specs=[pl.BlockSpec(memory_space=pltpu.SMEM)]
        + [pl.BlockSpec(memory_space=pltpu.VMEM)] * len(grams),
        out_specs=pl.BlockSpec(memory_space=pltpu.VMEM),
        out_shape=jax.ShapeDtypeStruct((tokens, 1), F32),
        cost_estimate=BRIEF,
        name="clip_factor",
    )(at, *grams)


def plus(a, b):
    return (a.astype(F32) + b.astype(F32)).astype(BF16)


def pipelined(inputs, out_grad, weight, noise):
    n = 4
    m, h = lax.axis_index("mp"), lax.axis_index("hidden")
    at = jnp.stack([h // 2, m // 2, h, m]).astype(jnp.int32)
    d_all, ff_all = inputs.shape[1] * n, out_grad.shape[1] * n
    tokens = inputs.shape[0] * n
    clip = math.sqrt(SEQ * d_all * ff_all)
    hold = lax.optimization_barrier

    g_side = swap(out_grad, 1)
    g_far = swap(out_grad, 2)
    x_side = along(inputs, OUTER)
    x_mid = middle(inputs)
    features, units = gram_pairs(inputs), gram_pairs(out_grad)
    pairs = features.shape[0]
    grams = along(jnp.concatenate([features, units]), OUTER)
    weight, g_side, features, units = hold((weight, g_side, features, units))


    def out_grad_rows(half):
        def place(at, pieces):
            core, near = at[3] & 1, half(at) == at[0]

            def slot(block_core):
                return jnp.where(near, (block_core ^ at[2] ^ 1) & 1, block_core ^ at[0] ^ 1)

            return [(None, slot(core), 0, pieces[0]), (None, slot(1 - core), 0, pieces[1])]

        return place

    def near_rows(at, pieces):
        slot = (at[2] ^ at[3]) & 1
        return [(None, slot, 0, pieces[0]), (None, 1 - slot, 0, pieces[1])]

    def far_rows(at, pieces):
        slot = (at[0] ^ at[3]) & 1
        inner = (at[2] == 1) | (at[2] == 2)
        outer = jnp.logical_not(inner)
        return [
            (inner, slot, 0, pieces[0]),
            (outer, slot, 0, pieces[1]),
            (inner, 1 - slot, 1, pieces[2]),
            (outer, 1 - slot, 1, pieces[3]),
        ]

    def plainly(at, first, second, merges, products):
        products[0][...] = first.astype(BF16)
        products[1][...] = second.astype(BF16)

    def in_grad_order(at, first, second, merges, products):
        near_first = at[0] == at[1]

        @pl.when(near_first)
        def _():
            products[0][...], products[1][...] = first.astype(BF16), second.astype(BF16)
            products[2][...], products[3][...] = merges[0][...], merges[1][...]

        @pl.when(jnp.logical_not(near_first))
        def _():
            products[0][...], products[1][...] = merges[0][...], merges[1][...]
            products[2][...], products[3][...] = first.astype(BF16), second.astype(BF16)

    def rows_here(share, before):
        return pair_matmul(
            at, [out_grad, g_side], weight, out_grad_rows(lambda at: at[1]), True, plainly, 2, [], [units],
            "in_grad_here", share=share, before=before,
        )

    x_side, x_mid, grams, *qa = hold((x_side, x_mid, grams, *rows_here((0, 5), ())))
    x_mid2 = middle(x_side)
    x_out = along(x_mid, OUTER)
    qa0, qa1, w = rows_here((5, 8), qa)
    pa0, pa1 = pair_matmul(
        at, [inputs, x_side], w, near_rows, False, plainly, 2, [], [], "outputs_near"
    )
    g_far, pa1, x_mid2, x_out, grams = hold((g_far, pa1, x_mid2, x_out, grams))
    features = jnp.concatenate([features, grams[:pairs]])
    units = plus(units, grams[pairs:])
    grams = along(jnp.concatenate([features, units]), [(i, i ^ 2) for i in range(n)])
    g_far_side = swap(g_far, 1)
    x_out2 = along(x_mid2, OUTWARD)
    pa1 = swap(pa1, 1)
    first, second, beside, own = pair_matmul(
        at, [g_far, g_far_side], w, out_grad_rows(lambda at: 1 - at[1]), True, in_grad_order, 4,
        [qa0, qa1], [pa0], "in_grad_there",
    )
    grams, first, pa1 = hold((grams, first, pa1))
    grams = jnp.concatenate(
        [features, grams[: 2 * pairs], plus(units, grams[2 * pairs :])]
    )
    others = [swap(grams, j) for j in range(1, n)]
    r1a = along(first, OUTER)

    def two(at, refs, outs):
        outs[0][...] = total(*refs).astype(BF16)

    narrow, wide = first.shape, pa0.shape
    (near_sum,) = add_up(at, two, [pa0, pa1], [], [wide], 2, "sums_near")
    pb0, pb1, x_far = pair_matmul(
        at, [x_mid, x_out, x_mid2, x_out2], w, far_rows, False, plainly, 2,
        [], [first, near_sum], "outputs_far", keep=True,
    )
    factor = make_factor(at, [grams, *others], clip, pairs, tokens)
    r1a, pb1, factor = hold((r1a, pb1, factor))
    pb1 = swap(pb1, 1)

    (r2a,) = add_up(at, two, [first, r1a], [], [narrow], 2, "sums_now")
    pb1, r2a = hold((pb1, r2a))
    r2a = middle(r2a)
    r1b = along(second, OUTER)

    def for_others(at, refs, outs):
        far = total(refs[1], refs[2])
        outs[0][...] = jnp.where(at[0] == at[1], far, refs[0][...].astype(F32)).astype(BF16)

    def if_same(at):
        return at[0] == at[1]

    def if_other(at):
        return at[0] != at[1]

    (other,) = add_up(
        at, for_others, [], [(if_other, near_sum), (if_same, pb0), (if_same, pb1)],
        [wide], 2, "sums_others",
    )
    theirs = swap(other, 2)

    def inner_only(at, ref):
        return jnp.where((at[2] == 1) | (at[2] == 2), ref[...].astype(F32), 0.0)

    def later(at, refs, outs):
        outs[0][...] = (refs[0][...].astype(F32) + inner_only(at, refs[1])).astype(BF16)
        outs[1][...] = total(refs[2], refs[3]).astype(BF16)

    def last_outputs(at, refs, outs):
        mine = jnp.where(at[0] == at[1], refs[1][...].astype(F32), total(*refs[2:]))
        outs[0][...] = (mine + refs[0][...].astype(F32)).astype(BF16)

    def last_in_grad(at, refs, outs):
        outs[0][...] = (total(*refs[:2]) + inner_only(at, refs[2])).astype(BF16)

    def block_of(at, j):
        return at[3] ^ j

    def slot_of(at, block):
        far = jnp.where(at[0] == 0, block, 3 - block)
        return jnp.where(block // 2 == at[0], (block ^ at[2]) & 1, far)

    xs = [(inputs, None), (x_side, None), (x_far, 0), (x_far, 1)]
    gs = [out_grad, g_side, g_far, g_far_side]
    gain = math.sqrt(d_all * ff_all) / clip
    facts = (slot_of, block_of, factor, noise, gain, tokens // SEQ)
    update = make_update(at, xs, gs, *facts, 0, 2, None, [other])
    r2a, r1b, update = hold((r2a, r1b, update))
    r3, r2b = add_up(at, later, [beside, r2a, second, r1b], [], [narrow, narrow], 2, "sums_later")
    r3 = along(r3, OUTER)
    r2b = middle(r2b)
    update = make_update(at, xs, gs, *facts, 1, 2, update)
    theirs, update = hold((theirs, update))
    (outputs,) = add_up(
        at, last_outputs, [theirs], [(if_same, near_sum), (if_other, pb0), (if_other, pb1)],
        [wide], 2, "sums_outputs",
    )
    r3, r2b, outputs = hold((r3, r2b, outputs))
    (in_grad,) = add_up(at, last_in_grad, [own, r3, r2b], [], [narrow], 2, "sums_in_grad")
    return outputs, in_grad, update


def plain(tokens, d_all, ff_all, inputs, out_grad, weight, noise):
    w = weight.astype(BF16)
    x = lax.all_gather(inputs, "hidden", axis=0, tiled=True)
    g = lax.all_gather(out_grad, "mp", axis=0, tiled=True)
    clip = math.sqrt(SEQ * d_all * ff_all)
    outputs = lax.psum_scatter(
        jnp.dot(x, w, preferred_element_type=F32), "mp", scatter_dimension=0, tiled=True
    )
    in_grad = lax.psum_scatter(
        lax.dot_general(g, w, (((1,), (1,)), ((), ())), preferred_element_type=F32),
        "hidden",
        scatter_dimension=0,
        tiled=True,
    )
    grams = lax.psum(gram(x), "mp") * lax.psum(gram(g), "hidden")
    factor = jnp.minimum(1.0, clip / jnp.sqrt(jnp.sum(grams, axis=(1, 2)) + 1e-06))
    none = lambda at, j: 0
    update = make_update(
        jnp.zeros((1,), jnp.int32),
        [(x, None)],
        [g],
        none,
        none,
        jnp.repeat(factor, SEQ)[:, None],
        noise,
        math.sqrt(d_all * ff_all) / clip,
        tokens // SEQ,
    )
    return outputs.astype(BF16), in_grad.astype(BF16), update


def solution(mesh):
    mp, hidden = mesh.shape["mp"], mesh.shape["hidden"]

    def shards(inputs, out_grad, weight, noise):
        if mp == hidden == 4 and inputs.shape[0] % (2 * SEQ) == 0:
            return pipelined(inputs, out_grad, weight, noise)
        return plain(
            inputs.shape[0] * hidden,
            inputs.shape[1] * mp,
            out_grad.shape[1] * hidden,
            inputs,
            out_grad,
            weight,
            noise,
        )

    in_specs = (
        P(("groups", "hidden"), "mp"),
        P(("groups", "mp"), "hidden"),
        P("mp", "hidden"),
        P(None, ("groups", "mp"), "hidden"),
    )
    out_specs = (
        P(("groups", "mp"), "hidden"),
        P(("groups", "hidden"), "mp"),
        P("mp", ("groups", "hidden")),
    )
    return jax.shard_map(shards, mesh=mesh, in_specs=in_specs, out_specs=out_specs, check_vma=False)
```

```python
import math

import jax
import jax.numpy as jnp
from jax import lax
from jax.experimental import pallas as pl
from jax.experimental.pallas import tpu as pltpu
from jax.sharding import PartitionSpec as P

SEQ = 64
NOISE_BAND = 0.6
NOISE_SCALE = 4.0
VMEM = 63 * 1024 * 1024
F32 = jnp.float32
BF16 = jnp.bfloat16
ANY = pl.BlockSpec(memory_space=pl.ANY)
BRIEF = pl.CostEstimate(flops=1, bytes_accessed=1, transcendentals=0)


def params(dims):
    return pltpu.CompilerParams(
        vmem_limit_bytes=VMEM, dimension_semantics=("arbitrary",) * dims
    )


def whole(shape):
    return pl.BlockSpec(shape, lambda *_: (0,) * len(shape))


def pair_kernel(transposed, place, finish, count, merged, extra, keep, at, *refs):
    pieces, w = refs[:count], refs[count]
    merges = refs[count + 1 : count + 1 + merged]
    *products, rows = refs[count + 1 + merged + extra :]
    kept = products.pop() if keep else None
    r = rows.shape[0] // 2

    @pl.when(pl.program_id(0) == 0)
    def _():
        for cond, slot, spot, piece in place(at, pieces):

            def put(slot=slot, spot=spot, piece=piece):
                rows[pl.ds(pl.multiple_of(slot * r, r), r), :] = piece[...]
                if keep:
                    kept[spot] = piece[...]

            if cond is None:
                put()
            else:
                pl.when(cond)(put)

    tile = w[...]
    if tile.dtype != BF16:
        tile = tile.astype(BF16)
        products[-1][...] = tile
    dims = (((1,), (1 if transposed else 0,)), ((), ()))
    total = lax.dot_general(rows[...], tile, dims, preferred_element_type=F32)
    finish(at, total[:r], total[r:], merges, products)


def pair_matmul(
    at, pieces, w, place, transposed, finish, outs, merges, after, name, keep=False, share=(0, 8), before=()
):
    r, depth = pieces[0].shape
    width = w.shape[0] if transposed else w.shape[1]
    cast = w.dtype != BF16
    tile = min(256 if cast else 512 if transposed else 1024, width)
    skip = width // tile * share[0] // 8
    steps = width // tile * share[1] // 8 - skip
    w_spec = (
        pl.BlockSpec((tile, depth), lambda i: (i + skip, 0))
        if transposed
        else pl.BlockSpec((depth, tile), lambda i: (0, i + skip))
    )
    extra = [*before, *after]
    count = len(pieces)
    first_extra = count + 2 + len(merges)
    product = pl.BlockSpec((r, tile), lambda i: (0, i + skip))
    kernel = lambda *refs: pair_kernel(
        transposed, place, finish, count, len(merges), len(extra), keep, *refs
    )
    return pl.pallas_call(
        kernel,
        grid=(steps,),
        in_specs=[pl.BlockSpec(memory_space=pltpu.SMEM)]
        + [whole((r, depth))] * count
        + [w_spec]
        + [product] * len(merges)
        + [ANY] * len(extra),
        out_specs=[product] * outs + [w_spec] * cast + [whole((2, r, depth))] * keep,
        scratch_shapes=[pltpu.VMEM((2 * r, depth), BF16)],
        out_shape=[jax.ShapeDtypeStruct((r, width), BF16)] * outs
        + [jax.ShapeDtypeStruct(w.shape, BF16)] * cast
        + [jax.ShapeDtypeStruct((2, r, depth), BF16)] * keep,
        input_output_aliases={first_extra + i: i for i in range(len(before))},
        compiler_params=params(1),
        cost_estimate=BRIEF,
        name=name,
    )(at, *pieces, w, *merges, *extra)


def update_kernel(gain, count, nx, ng, extra, slot_of, block_of, at, factor, *refs):
    xs, gs, noise = refs[:nx], refs[nx : nx + ng], refs[nx + ng]
    out, scaled, rows = refs[nx + ng + 1 + extra :]
    rx, rg = rows.shape[0] // nx, scaled.shape[0] // ng

    @pl.when(pl.program_id(0) == 0)
    def _():
        for j, g in enumerate(gs):
            block = block_of(at, j)
            source, target = block * rg, slot_of(at, block) * rg
            for t in range(0, rg, SEQ):
                scale = factor[pl.ds(pl.multiple_of(source + t, SEQ), SEQ), :]
                scaled[pl.ds(pl.multiple_of(target + t, SEQ), SEQ), :] = (
                    g[t : t + SEQ, :].astype(F32) * scale
                ).astype(BF16)

    for j, x in enumerate(xs):
        rows[j * rx : (j + 1) * rx, :] = x[...].reshape(rx, -1)
    step = min(1024, out.shape[1])
    for j in range(0, out.shape[1], step):
        span = pl.ds(j, step)
        grad = lax.dot_general(
            rows[...], scaled[:, span], (((0,), (0,)), ((), ())), preferred_element_type=F32
        )
        band = noise[0, :, span].astype(F32) - NOISE_BAND * noise[1, :, span].astype(F32)
        out[:, span] = (grad * gain + NOISE_SCALE * band) * (1.0 / count)


def make_update(
    at, xs, gs, slot_of, block_of, factor, noise, gain, count, part=0, parts=1, before=None, after=()
):
    tokens = factor.shape[0]
    depth, whole_width = noise.shape[1:]
    width = whole_width // parts
    tile = min(512, depth)
    rx, rg = tokens // len(xs), tokens // len(gs)
    extra = ([] if before is None else [before]) + list(after)

    def x_spec(lead):
        if lead is None:
            return pl.BlockSpec((rx, tile), lambda i: (0, i))
        return pl.BlockSpec((1, rx, tile), lambda i: (lead, 0, i))

    def kernel(*refs):
        update_kernel(gain, count, len(xs), len(gs), len(extra), slot_of, block_of, *refs)

    return pl.pallas_call(
        kernel,
        grid=(depth // tile,),
        in_specs=[pl.BlockSpec(memory_space=pltpu.SMEM), whole((tokens, 1))]
        + [x_spec(lead) for _, lead in xs]
        + [pl.BlockSpec((rg, width), lambda i: (0, part))] * len(gs)
        + [pl.BlockSpec((2, tile, width), lambda i: (0, i, part))]
        + [ANY] * len(extra),
        out_specs=pl.BlockSpec((tile, width), lambda i: (i, part)),
        out_shape=jax.ShapeDtypeStruct((depth, whole_width), F32),
        scratch_shapes=[pltpu.VMEM((tokens, width), BF16), pltpu.VMEM((tokens, tile), BF16)],
        input_output_aliases={} if before is None else {3 + len(xs) + len(gs): 0},
        compiler_params=params(1),
        cost_estimate=BRIEF,
        name="update",
    )(at, factor, *[x for x, _ in xs], *gs, noise, *extra)


def add_kernel(sums, ins, at, *refs):
    sums(at, refs[:ins], refs[ins:])


def add_up(at, sums, arrays, choices, outs, steps, name):
    def band(shape, cond=None):
        def index(i, at):
            return (i if cond is None else jnp.where(cond(at), i, 0), 0)

        return pl.BlockSpec((shape[0] // steps, shape[1]), index)

    arrays, chosen = list(arrays), [x for _, x in choices]
    return pl.pallas_call(
        lambda *refs: add_kernel(sums, len(arrays) + len(chosen), *refs),
        grid_spec=pltpu.PrefetchScalarGridSpec(
            num_scalar_prefetch=1,
            grid=(steps,),
            in_specs=[band(x.shape) for x in arrays] + [band(x.shape, c) for c, x in choices],
            out_specs=[band(shape) for shape in outs],
        ),
        out_shape=[jax.ShapeDtypeStruct(shape, BF16) for shape in outs],
        compiler_params=params(1),
        cost_estimate=BRIEF,
        name=name,
    )(at, *arrays, *chosen)


def total(*refs):
    return sum(ref[...].astype(F32) for ref in refs)


OUTER = [(0, 1), (1, 0), (2, 3), (3, 2)]
INWARD = [(0, 1), (3, 2)]
OUTWARD = [(1, 0), (2, 3)]


def along(value, pairs):
    return lax.ppermute(value, "hidden", pairs)


def middle(value):
    pairs = [
        (m * 4 + h, m * 4 + 3 - h if h in (1, 2) else (m ^ 1) * 4 + h)
        for m in range(4)
        for h in range(4)
    ]
    return lax.ppermute(value, ("mp", "hidden"), pairs)


def swap(value, bit):
    return lax.ppermute(value, "mp", [(i, i ^ bit) for i in range(4)])


def gram(rows):
    blocks = rows.reshape(-1, SEQ, rows.shape[1])
    return jnp.einsum("bsd,btd->bst", blocks, blocks, preferred_element_type=F32)


def gram_kernel(*refs):
    *arrays, out = refs
    pairs = out.shape[0] // len(arrays)
    for i, rows in enumerate(arrays):
        for e in range(2 * pairs):
            block = rows[e * SEQ : (e + 1) * SEQ, :]
            square = lax.dot_general(
                block, block, (((1,), (1,)), ((), ())), preferred_element_type=F32
            )
            side = e % 2 * SEQ
            out[i * pairs + e // 2, :, side : side + SEQ] = square.astype(BF16)


def gram_pairs(*arrays):
    pairs = arrays[0].shape[0] // SEQ // 2
    return pl.pallas_call(
        gram_kernel,
        in_specs=[pl.BlockSpec(memory_space=pltpu.VMEM)] * len(arrays),
        out_specs=pl.BlockSpec(memory_space=pltpu.VMEM),
        out_shape=jax.ShapeDtypeStruct((len(arrays) * pairs, SEQ, 2 * SEQ), BF16),
        compiler_params=pltpu.CompilerParams(vmem_limit_bytes=VMEM),
        cost_estimate=BRIEF,
        name="gram",
    )(*arrays)


def factor_kernel(clip, pairs, n, at, *refs):
    *grams, out = refs
    h, m = at[2], at[3]
    r = out.shape[0] // n
    lane = lax.broadcasted_iota(jnp.int32, (1, 2 * SEQ), 1)
    for i, gram in enumerate(grams):
        block = m ^ i
        for p in range(pairs):
            spot = (block ^ h) * pairs + p
            feature = sum(g[spot].astype(F32) for g in grams)
            products = feature * gram[n * pairs + p].astype(F32)
            sums = jnp.sum(products, axis=0, keepdims=True)
            for side in range(2):
                square = jnp.sum(
                    jnp.where(lane // SEQ == side, sums, 0.0), axis=1, keepdims=True
                )
                factor = jnp.minimum(1.0, clip / jnp.sqrt(square + 1e-06))
                start = pl.multiple_of(block * r + (2 * p + side) * SEQ, SEQ)
                out[pl.ds(start, SEQ), :] = jnp.broadcast_to(factor, (SEQ, 1))


def make_factor(at, grams, clip, pairs, tokens):
    return pl.pallas_call(
        lambda *refs: factor_kernel(clip, pairs, len(grams), *refs),
        in_specs=[pl.BlockSpec(memory_space=pltpu.SMEM)]
        + [pl.BlockSpec(memory_space=pltpu.VMEM)] * len(grams),
        out_specs=pl.BlockSpec(memory_space=pltpu.VMEM),
        out_shape=jax.ShapeDtypeStruct((tokens, 1), F32),
        cost_estimate=BRIEF,
        name="clip_factor",
    )(at, *grams)


def plus(a, b):
    return (a.astype(F32) + b.astype(F32)).astype(BF16)


def pipelined(inputs, out_grad, weight, noise):
    n = 4
    m, h = lax.axis_index("mp"), lax.axis_index("hidden")
    at = jnp.stack([h // 2, m // 2, h, m]).astype(jnp.int32)
    d_all, ff_all = inputs.shape[1] * n, out_grad.shape[1] * n
    tokens = inputs.shape[0] * n
    clip = math.sqrt(SEQ * d_all * ff_all)
    hold = lax.optimization_barrier

    g_side = swap(out_grad, 1)
    g_far = swap(out_grad, 2)
    x_side = along(inputs, OUTER)
    x_mid = middle(inputs)
    grams = gram_pairs(inputs, out_grad)
    pairs = grams.shape[0] // 2
    features, units = grams[:pairs], grams[pairs:]
    weight, g_side, first_grams = hold((weight, g_side, grams))
    grams = along(grams, OUTER)


    def out_grad_rows(half):
        def place(at, pieces):
            core, near = at[3] & 1, half(at) == at[0]

            def slot(block_core):
                return jnp.where(near, (block_core ^ at[2] ^ 1) & 1, block_core ^ at[0] ^ 1)

            return [(None, slot(core), 0, pieces[0]), (None, slot(1 - core), 0, pieces[1])]

        return place

    def near_rows(at, pieces):
        slot = (at[2] ^ at[3]) & 1
        return [(None, slot, 0, pieces[0]), (None, 1 - slot, 0, pieces[1])]

    def far_rows(at, pieces):
        slot = (at[0] ^ at[3]) & 1
        inner = (at[2] == 1) | (at[2] == 2)
        outer = jnp.logical_not(inner)
        return [
            (inner, slot, 0, pieces[0]),
            (outer, slot, 0, pieces[1]),
            (inner, 1 - slot, 1, pieces[2]),
            (outer, 1 - slot, 1, pieces[3]),
        ]

    def plainly(at, first, second, merges, products):
        products[0][...] = first.astype(BF16)
        products[1][...] = second.astype(BF16)

    def in_grad_order(at, first, second, merges, products):
        near_first = at[0] == at[1]

        @pl.when(near_first)
        def _():
            products[0][...], products[1][...] = first.astype(BF16), second.astype(BF16)
            products[2][...], products[3][...] = merges[0][...], merges[1][...]

        @pl.when(jnp.logical_not(near_first))
        def _():
            products[0][...], products[1][...] = merges[0][...], merges[1][...]
            products[2][...], products[3][...] = first.astype(BF16), second.astype(BF16)

    def rows_here(share, before):
        return pair_matmul(
            at, [out_grad, g_side], weight, out_grad_rows(lambda at: at[1]), True, plainly, 2, [], [first_grams],
            "in_grad_here", share=share, before=before,
        )

    x_side, x_mid, grams, *qa = hold((x_side, x_mid, grams, *rows_here((0, 6), ())))
    x_mid2 = middle(x_side)
    x_out = along(x_mid, OUTER)
    qa0, qa1, w = rows_here((6, 8), qa)
    pa0, pa1 = pair_matmul(
        at, [inputs, x_side], w, near_rows, False, plainly, 2, [], [], "outputs_near"
    )
    g_far, pa1, x_mid2, x_out, grams = hold((g_far, pa1, x_mid2, x_out, grams))
    features = jnp.concatenate([features, grams[:pairs]])
    units = plus(units, grams[pairs:])
    grams = along(jnp.concatenate([features, units]), [(i, i ^ 2) for i in range(n)])
    g_far_side = swap(g_far, 1)
    x_out2 = along(x_mid2, OUTWARD)
    pa1 = swap(pa1, 1)
    first, second, beside, own = pair_matmul(
        at, [g_far, g_far_side], w, out_grad_rows(lambda at: 1 - at[1]), True, in_grad_order, 4,
        [qa0, qa1], [pa0], "in_grad_there",
    )
    grams, first, pa1 = hold((grams, first, pa1))
    grams = jnp.concatenate(
        [features, grams[: 2 * pairs], plus(units, grams[2 * pairs :])]
    )
    others = [swap(grams, j) for j in range(1, n)]
    r1a = along(first, INWARD)

    def two(at, refs, outs):
        outs[0][...] = total(*refs).astype(BF16)

    narrow, wide = first.shape, pa0.shape
    pb0, pb1, x_far = pair_matmul(
        at, [x_mid, x_out, x_mid2, x_out2], w, far_rows, False, plainly, 2,
        [], [first], "outputs_far", keep=True,
    )
    factor = make_factor(at, [grams, *others], clip, pairs, tokens)
    r1a, pb1, factor = hold((r1a, pb1, factor))
    pb1 = swap(pb1, 1)

    (r2a,) = add_up(at, two, [first, r1a], [], [narrow], 2, "sums_now")
    pb1, r2a = hold((pb1, r2a))
    r2a = middle(r2a)
    r1b = along(second, OUTER)

    def either(cond, pair, other):
        return jnp.where(cond, total(*pair), total(*other))

    def for_others(at, refs, outs):
        outs[0][...] = either(at[0] == at[1], refs[2:], refs[:2]).astype(BF16)

    def if_same(at):
        return at[0] == at[1]

    def if_other(at):
        return at[0] != at[1]

    (other,) = add_up(
        at, for_others, [], [(if_other, pa0), (if_other, pa1), (if_same, pb0), (if_same, pb1)],
        [wide], 2, "sums_others",
    )
    theirs = swap(other, 2)

    def inner_only(at, ref):
        return jnp.where((at[2] == 1) | (at[2] == 2), ref[...].astype(F32), 0.0)

    def later(at, refs, outs):
        outs[0][...] = (refs[0][...].astype(F32) + inner_only(at, refs[1])).astype(BF16)
        outs[1][...] = total(refs[2], refs[3]).astype(BF16)

    def last_outputs(at, refs, outs):
        mine = either(at[0] == at[1], refs[1:3], refs[3:])
        outs[0][...] = (mine + refs[0][...].astype(F32)).astype(BF16)

    def last_in_grad(at, refs, outs):
        outs[0][...] = (total(*refs[:2]) + inner_only(at, refs[2])).astype(BF16)

    def block_of(at, j):
        return at[3] ^ j

    def slot_of(at, block):
        far = jnp.where(at[0] == 0, block, 3 - block)
        return jnp.where(block // 2 == at[0], (block ^ at[2]) & 1, far)

    xs = [(inputs, None), (x_side, None), (x_far, 0), (x_far, 1)]
    gs = [out_grad, g_side, g_far, g_far_side]
    gain = math.sqrt(d_all * ff_all) / clip
    facts = (slot_of, block_of, factor, noise, gain, tokens // SEQ)
    update = make_update(at, xs, gs, *facts, 0, 2, None, [other])
    r2a, r1b, update = hold((r2a, r1b, update))
    r3, r2b = add_up(at, later, [beside, r2a, second, r1b], [], [narrow, narrow], 2, "sums_later")
    r3 = along(r3, OUTER)
    r2b = middle(r2b)
    update = make_update(at, xs, gs, *facts, 1, 2, update)
    theirs, update = hold((theirs, update))
    (outputs,) = add_up(
        at, last_outputs, [theirs],
        [(if_same, pa0), (if_same, pa1), (if_other, pb0), (if_other, pb1)], [wide], 2, "sums_outputs",
    )
    r3, r2b, outputs = hold((r3, r2b, outputs))
    (in_grad,) = add_up(at, last_in_grad, [own, r3, r2b], [], [narrow], 2, "sums_in_grad")
    return outputs, in_grad, update


def plain(tokens, d_all, ff_all, inputs, out_grad, weight, noise):
    w = weight.astype(BF16)
    x = lax.all_gather(inputs, "hidden", axis=0, tiled=True)
    g = lax.all_gather(out_grad, "mp", axis=0, tiled=True)
    clip = math.sqrt(SEQ * d_all * ff_all)
    outputs = lax.psum_scatter(
        jnp.dot(x, w, preferred_element_type=F32), "mp", scatter_dimension=0, tiled=True
    )
    in_grad = lax.psum_scatter(
        lax.dot_general(g, w, (((1,), (1,)), ((), ())), preferred_element_type=F32),
        "hidden",
        scatter_dimension=0,
        tiled=True,
    )
    grams = lax.psum(gram(x), "mp") * lax.psum(gram(g), "hidden")
    factor = jnp.minimum(1.0, clip / jnp.sqrt(jnp.sum(grams, axis=(1, 2)) + 1e-06))
    none = lambda at, j: 0
    update = make_update(
        jnp.zeros((1,), jnp.int32),
        [(x, None)],
        [g],
        none,
        none,
        jnp.repeat(factor, SEQ)[:, None],
        noise,
        math.sqrt(d_all * ff_all) / clip,
        tokens // SEQ,
    )
    return outputs.astype(BF16), in_grad.astype(BF16), update


def solution(mesh):
    mp, hidden = mesh.shape["mp"], mesh.shape["hidden"]

    def shards(inputs, out_grad, weight, noise):
        if mp == hidden == 4 and inputs.shape[0] % (2 * SEQ) == 0:
            return pipelined(inputs, out_grad, weight, noise)
        return plain(
            inputs.shape[0] * hidden,
            inputs.shape[1] * mp,
            out_grad.shape[1] * hidden,
            inputs,
            out_grad,
            weight,
            noise,
        )

    in_specs = (
        P(("groups", "hidden"), "mp"),
        P(("groups", "mp"), "hidden"),
        P("mp", "hidden"),
        P(None, ("groups", "mp"), "hidden"),
    )
    out_specs = (
        P(("groups", "mp"), "hidden"),
        P(("groups", "hidden"), "mp"),
        P("mp", ("groups", "hidden")),
    )
    return jax.shard_map(shards, mesh=mesh, in_specs=in_specs, out_specs=out_specs, check_vma=False)
```

```python
import math

import jax
import jax.numpy as jnp
from jax import lax
from jax.experimental import pallas as pl
from jax.experimental.pallas import tpu as pltpu
from jax.sharding import PartitionSpec as P

SEQ = 64
NOISE_BAND = 0.6
NOISE_SCALE = 4.0
VMEM = 63 * 1024 * 1024
F32 = jnp.float32
BF16 = jnp.bfloat16
ANY = pl.BlockSpec(memory_space=pl.ANY)
BRIEF = pl.CostEstimate(flops=1, bytes_accessed=1, transcendentals=0)


def params(dims):
    return pltpu.CompilerParams(
        vmem_limit_bytes=VMEM, dimension_semantics=("arbitrary",) * dims
    )


def whole(shape):
    return pl.BlockSpec(shape, lambda *_: (0,) * len(shape))


def pair_kernel(transposed, place, finish, count, merged, extra, keep, at, *refs):
    pieces, w = refs[:count], refs[count]
    merges = refs[count + 1 : count + 1 + merged]
    *products, rows = refs[count + 1 + merged + extra :]
    kept = products.pop() if keep else None
    r = rows.shape[0] // 2

    @pl.when(pl.program_id(0) == 0)
    def _():
        for cond, slot, spot, piece in place(at, pieces):

            def put(slot=slot, spot=spot, piece=piece):
                rows[pl.ds(pl.multiple_of(slot * r, r), r), :] = piece[...]
                if keep:
                    kept[spot] = piece[...]

            if cond is None:
                put()
            else:
                pl.when(cond)(put)

    tile = w[...]
    if tile.dtype != BF16:
        tile = tile.astype(BF16)
        products[-1][...] = tile
    dims = (((1,), (1 if transposed else 0,)), ((), ()))
    total = lax.dot_general(rows[...], tile, dims, preferred_element_type=F32)
    finish(at, total[:r], total[r:], merges, products)


def pair_matmul(
    at, pieces, w, place, transposed, finish, outs, merges, after, name, keep=False, share=(0, 8), before=()
):
    r, depth = pieces[0].shape
    width = w.shape[0] if transposed else w.shape[1]
    cast = w.dtype != BF16
    tile = min(256 if cast else 512 if transposed else 1024, width)
    skip = width // tile * share[0] // 8
    steps = width // tile * share[1] // 8 - skip
    w_spec = (
        pl.BlockSpec((tile, depth), lambda i: (i + skip, 0))
        if transposed
        else pl.BlockSpec((depth, tile), lambda i: (0, i + skip))
    )
    extra = [*before, *after]
    count = len(pieces)
    first_extra = count + 2 + len(merges)
    product = pl.BlockSpec((r, tile), lambda i: (0, i + skip))
    kernel = lambda *refs: pair_kernel(
        transposed, place, finish, count, len(merges), len(extra), keep, *refs
    )
    return pl.pallas_call(
        kernel,
        grid=(steps,),
        in_specs=[pl.BlockSpec(memory_space=pltpu.SMEM)]
        + [whole((r, depth))] * count
        + [w_spec]
        + [product] * len(merges)
        + [ANY] * len(extra),
        out_specs=[product] * outs + [w_spec] * cast + [whole((2, r, depth))] * keep,
        scratch_shapes=[pltpu.VMEM((2 * r, depth), BF16)],
        out_shape=[jax.ShapeDtypeStruct((r, width), BF16)] * outs
        + [jax.ShapeDtypeStruct(w.shape, BF16)] * cast
        + [jax.ShapeDtypeStruct((2, r, depth), BF16)] * keep,
        input_output_aliases={first_extra + i: i for i in range(len(before))},
        compiler_params=params(1),
        cost_estimate=BRIEF,
        name=name,
    )(at, *pieces, w, *merges, *extra)


def update_kernel(gain, count, nx, ng, extra, slot_of, block_of, at, factor, *refs):
    xs, gs, noise = refs[:nx], refs[nx : nx + ng], refs[nx + ng]
    out, scaled, rows = refs[nx + ng + 1 + extra :]
    rx, rg = rows.shape[0] // nx, scaled.shape[0] // ng

    @pl.when(pl.program_id(0) == 0)
    def _():
        for j, g in enumerate(gs):
            block = block_of(at, j)
            source, target = block * rg, slot_of(at, block) * rg
            for t in range(0, rg, SEQ):
                scale = factor[pl.ds(pl.multiple_of(source + t, SEQ), SEQ), :]
                scaled[pl.ds(pl.multiple_of(target + t, SEQ), SEQ), :] = (
                    g[t : t + SEQ, :].astype(F32) * scale
                ).astype(BF16)

    for j, x in enumerate(xs):
        rows[j * rx : (j + 1) * rx, :] = x[...].reshape(rx, -1)
    step = min(1024, out.shape[1])
    for j in range(0, out.shape[1], step):
        span = pl.ds(j, step)
        grad = lax.dot_general(
            rows[...], scaled[:, span], (((0,), (0,)), ((), ())), preferred_element_type=F32
        )
        band = noise[0, :, span].astype(F32) - NOISE_BAND * noise[1, :, span].astype(F32)
        out[:, span] = (grad * gain + NOISE_SCALE * band) * (1.0 / count)


def make_update(
    at, xs, gs, slot_of, block_of, factor, noise, gain, count, part=0, parts=1, before=None, after=()
):
    tokens = factor.shape[0]
    depth, whole_width = noise.shape[1:]
    width = whole_width // parts
    tile = min(512, depth)
    rx, rg = tokens // len(xs), tokens // len(gs)
    extra = ([] if before is None else [before]) + list(after)

    def x_spec(lead):
        if lead is None:
            return pl.BlockSpec((rx, tile), lambda i: (0, i))
        return pl.BlockSpec((1, rx, tile), lambda i: (lead, 0, i))

    def kernel(*refs):
        update_kernel(gain, count, len(xs), len(gs), len(extra), slot_of, block_of, *refs)

    return pl.pallas_call(
        kernel,
        grid=(depth // tile,),
        in_specs=[pl.BlockSpec(memory_space=pltpu.SMEM), whole((tokens, 1))]
        + [x_spec(lead) for _, lead in xs]
        + [pl.BlockSpec((rg, width), lambda i: (0, part))] * len(gs)
        + [pl.BlockSpec((2, tile, width), lambda i: (0, i, part))]
        + [ANY] * len(extra),
        out_specs=pl.BlockSpec((tile, width), lambda i: (i, part)),
        out_shape=jax.ShapeDtypeStruct((depth, whole_width), F32),
        scratch_shapes=[pltpu.VMEM((tokens, width), BF16), pltpu.VMEM((tokens, tile), BF16)],
        input_output_aliases={} if before is None else {3 + len(xs) + len(gs): 0},
        compiler_params=params(1),
        cost_estimate=BRIEF,
        name="update",
    )(at, factor, *[x for x, _ in xs], *gs, noise, *extra)


def add_kernel(sums, ins, at, *refs):
    sums(at, refs[:ins], refs[ins:])


def add_up(at, sums, arrays, choices, outs, steps, name):
    def band(shape, cond=None):
        def index(i, at):
            return (i if cond is None else jnp.where(cond(at), i, 0), 0)

        return pl.BlockSpec((shape[0] // steps, shape[1]), index)

    arrays, chosen = list(arrays), [x for _, x in choices]
    return pl.pallas_call(
        lambda *refs: add_kernel(sums, len(arrays) + len(chosen), *refs),
        grid_spec=pltpu.PrefetchScalarGridSpec(
            num_scalar_prefetch=1,
            grid=(steps,),
            in_specs=[band(x.shape) for x in arrays] + [band(x.shape, c) for c, x in choices],
            out_specs=[band(shape) for shape in outs],
        ),
        out_shape=[jax.ShapeDtypeStruct(shape, BF16) for shape in outs],
        compiler_params=params(1),
        cost_estimate=BRIEF,
        name=name,
    )(at, *arrays, *chosen)


def total(*refs):
    return sum(ref[...].astype(F32) for ref in refs)


OUTER = [(0, 1), (1, 0), (2, 3), (3, 2)]
INWARD = [(0, 1), (3, 2)]
OUTWARD = [(1, 0), (2, 3)]


def along(value, pairs):
    return lax.ppermute(value, "hidden", pairs)


def middle(value):
    pairs = [
        (m * 4 + h, m * 4 + 3 - h if h in (1, 2) else (m ^ 1) * 4 + h)
        for m in range(4)
        for h in range(4)
    ]
    return lax.ppermute(value, ("mp", "hidden"), pairs)


def swap(value, bit):
    return lax.ppermute(value, "mp", [(i, i ^ bit) for i in range(4)])


def gram(rows):
    blocks = rows.reshape(-1, SEQ, rows.shape[1])
    return jnp.einsum("bsd,btd->bst", blocks, blocks, preferred_element_type=F32)


def gram_kernel(*refs):
    *arrays, out = refs
    pairs = out.shape[0] // len(arrays)
    for i, rows in enumerate(arrays):
        for e in range(2 * pairs):
            block = rows[e * SEQ : (e + 1) * SEQ, :]
            square = lax.dot_general(
                block, block, (((1,), (1,)), ((), ())), preferred_element_type=F32
            )
            side = e % 2 * SEQ
            out[i * pairs + e // 2, :, side : side + SEQ] = square.astype(BF16)


def gram_pairs(*arrays):
    pairs = arrays[0].shape[0] // SEQ // 2
    return pl.pallas_call(
        gram_kernel,
        in_specs=[pl.BlockSpec(memory_space=pltpu.VMEM)] * len(arrays),
        out_specs=pl.BlockSpec(memory_space=pltpu.VMEM),
        out_shape=jax.ShapeDtypeStruct((len(arrays) * pairs, SEQ, 2 * SEQ), BF16),
        compiler_params=pltpu.CompilerParams(vmem_limit_bytes=VMEM),
        cost_estimate=BRIEF,
        name="gram",
    )(*arrays)


def factor_kernel(clip, pairs, n, at, *refs):
    *grams, out = refs
    h, m = at[2], at[3]
    r = out.shape[0] // n
    lane = lax.broadcasted_iota(jnp.int32, (1, 2 * SEQ), 1)
    for i, gram in enumerate(grams):
        block = m ^ i
        for p in range(pairs):
            spot = (block ^ h) * pairs + p
            feature = sum(g[spot].astype(F32) for g in grams)
            products = feature * gram[n * pairs + p].astype(F32)
            sums = jnp.sum(products, axis=0, keepdims=True)
            for side in range(2):
                square = jnp.sum(
                    jnp.where(lane // SEQ == side, sums, 0.0), axis=1, keepdims=True
                )
                factor = jnp.minimum(1.0, clip / jnp.sqrt(jnp.maximum(square, 0.0) + 1e-06))
                start = pl.multiple_of(block * r + (2 * p + side) * SEQ, SEQ)
                out[pl.ds(start, SEQ), :] = jnp.broadcast_to(factor, (SEQ, 1))


def make_factor(at, grams, clip, pairs, tokens):
    return pl.pallas_call(
        lambda *refs: factor_kernel(clip, pairs, len(grams), *refs),
        in_specs=[pl.BlockSpec(memory_space=pltpu.SMEM)]
        + [pl.BlockSpec(memory_space=pltpu.VMEM)] * len(grams),
        out_specs=pl.BlockSpec(memory_space=pltpu.VMEM),
        out_shape=jax.ShapeDtypeStruct((tokens, 1), F32),
        cost_estimate=BRIEF,
        name="clip_factor",
    )(at, *grams)


def plus(a, b):
    return (a.astype(F32) + b.astype(F32)).astype(BF16)


def pipelined(inputs, out_grad, weight, noise):
    n = 4
    m, h = lax.axis_index("mp"), lax.axis_index("hidden")
    at = jnp.stack([h // 2, m // 2, h, m]).astype(jnp.int32)
    d_all, ff_all = inputs.shape[1] * n, out_grad.shape[1] * n
    tokens = inputs.shape[0] * n
    clip = math.sqrt(SEQ * d_all * ff_all)
    hold = lax.optimization_barrier

    g_side = swap(out_grad, 1)
    g_far = swap(out_grad, 2)
    x_side = along(inputs, OUTER)
    x_mid = middle(inputs)
    grams = gram_pairs(inputs, out_grad)
    pairs = grams.shape[0] // 2
    features, units = grams[:pairs], grams[pairs:]
    weight, g_side, first_grams = hold((weight, g_side, grams))
    grams = along(grams, OUTER)


    def out_grad_rows(half):
        def place(at, pieces):
            core, near = at[3] & 1, half(at) == at[0]

            def slot(block_core):
                return jnp.where(near, (block_core ^ at[2] ^ 1) & 1, block_core ^ at[0] ^ 1)

            return [(None, slot(core), 0, pieces[0]), (None, slot(1 - core), 0, pieces[1])]

        return place

    def near_rows(at, pieces):
        slot = (at[2] ^ at[3]) & 1
        return [(None, slot, 0, pieces[0]), (None, 1 - slot, 0, pieces[1])]

    def far_rows(at, pieces):
        slot = (at[0] ^ at[3]) & 1
        inner = (at[2] == 1) | (at[2] == 2)
        outer = jnp.logical_not(inner)
        return [
            (inner, slot, 0, pieces[0]),
            (outer, slot, 0, pieces[1]),
            (inner, 1 - slot, 1, pieces[2]),
            (outer, 1 - slot, 1, pieces[3]),
        ]

    def plainly(at, first, second, merges, products):
        products[0][...] = first.astype(BF16)
        products[1][...] = second.astype(BF16)

    def in_grad_order(at, first, second, merges, products):
        near_first = at[0] == at[1]

        @pl.when(near_first)
        def _():
            products[0][...], products[1][...] = first.astype(BF16), second.astype(BF16)
            products[2][...], products[3][...] = merges[0][...], merges[1][...]

        @pl.when(jnp.logical_not(near_first))
        def _():
            products[0][...], products[1][...] = merges[0][...], merges[1][...]
            products[2][...], products[3][...] = first.astype(BF16), second.astype(BF16)

    def rows_here(share, before):
        return pair_matmul(
            at, [out_grad, g_side], weight, out_grad_rows(lambda at: at[1]), True, plainly, 2, [], [first_grams],
            "in_grad_here", share=share, before=before,
        )

    x_side, x_mid, grams, *qa = hold((x_side, x_mid, grams, *rows_here((0, 6), ())))
    x_mid2 = middle(x_side)
    x_out = along(x_mid, OUTER)
    qa0, qa1, w = rows_here((6, 8), qa)
    pa0, pa1 = pair_matmul(
        at, [inputs, x_side], w, near_rows, False, plainly, 2, [], [], "outputs_near"
    )
    g_far, pa1, x_mid2, x_out, grams = hold((g_far, pa1, x_mid2, x_out, grams))
    features = jnp.concatenate([features, grams[:pairs]])
    units = plus(units, grams[pairs:])
    grams = along(jnp.concatenate([features, units]), [(i, i ^ 2) for i in range(n)])
    g_far_side = swap(g_far, 1)
    x_out2 = along(x_mid2, OUTWARD)
    pa1 = swap(pa1, 1)
    first, second, beside, own = pair_matmul(
        at, [g_far, g_far_side], w, out_grad_rows(lambda at: 1 - at[1]), True, in_grad_order, 4,
        [qa0, qa1], [pa0], "in_grad_there",
    )
    grams, first, pa1 = hold((grams, first, pa1))
    grams = jnp.concatenate(
        [features, grams[: 2 * pairs], plus(units, grams[2 * pairs :])]
    )
    others = [swap(grams, j) for j in range(1, n)]
    r1a = along(first, INWARD)

    def two(at, refs, outs):
        outs[0][...] = total(*refs).astype(BF16)

    narrow, wide = first.shape, pa0.shape
    pb0, pb1, x_far = pair_matmul(
        at, [x_mid, x_out, x_mid2, x_out2], w, far_rows, False, plainly, 2,
        [], [first], "outputs_far", keep=True,
    )
    factor = make_factor(at, [grams, *others], clip, pairs, tokens)
    r1a, pb1, factor = hold((r1a, pb1, factor))
    pb1 = swap(pb1, 1)

    (r2a,) = add_up(at, two, [first, r1a], [], [narrow], 2, "sums_now")
    pb1, r2a = hold((pb1, r2a))
    r2a = middle(r2a)
    r1b = along(second, OUTER)

    def either(cond, pair, other):
        return jnp.where(cond, total(*pair), total(*other))

    def for_others(at, refs, outs):
        outs[0][...] = either(at[0] == at[1], refs[2:], refs[:2]).astype(BF16)

    def if_same(at):
        return at[0] == at[1]

    def if_other(at):
        return at[0] != at[1]

    (other,) = add_up(
        at, for_others, [], [(if_other, pa0), (if_other, pa1), (if_same, pb0), (if_same, pb1)],
        [wide], 2, "sums_others",
    )
    theirs = swap(other, 2)

    def inner_only(at, ref):
        return jnp.where((at[2] == 1) | (at[2] == 2), ref[...].astype(F32), 0.0)

    def later(at, refs, outs):
        outs[0][...] = (refs[0][...].astype(F32) + inner_only(at, refs[1])).astype(BF16)
        outs[1][...] = total(refs[2], refs[3]).astype(BF16)

    def last(at, refs, outs):
        mine = either(at[0] == at[1], refs[4:6], refs[6:])
        outs[0][...] = (mine + refs[0][...].astype(F32)).astype(BF16)
        outs[1][...] = (total(*refs[1:3]) + inner_only(at, refs[3])).astype(BF16)

    def block_of(at, j):
        return at[3] ^ j

    def slot_of(at, block):
        far = jnp.where(at[0] == 0, block, 3 - block)
        return jnp.where(block // 2 == at[0], (block ^ at[2]) & 1, far)

    xs = [(inputs, None), (x_side, None), (x_far, 0), (x_far, 1)]
    gs = [out_grad, g_side, g_far, g_far_side]
    gain = math.sqrt(d_all * ff_all) / clip
    facts = (slot_of, block_of, factor, noise, gain, tokens // SEQ)
    update = make_update(at, xs, gs, *facts, 0, 2, None, [other])
    r2a, r1b, update = hold((r2a, r1b, update))
    r3, r2b = add_up(at, later, [beside, r2a, second, r1b], [], [narrow, narrow], 2, "sums_later")
    r3 = along(r3, OUTER)
    r2b = middle(r2b)
    update = make_update(at, xs, gs, *facts, 1, 2, update)
    r3, r2b, theirs, update = hold((r3, r2b, theirs, update))
    outputs, in_grad = add_up(
        at, last, [theirs, own, r3, r2b],
        [(if_same, pa0), (if_same, pa1), (if_other, pb0), (if_other, pb1)], [wide, narrow], 2, "sums_last",
    )
    return outputs, in_grad, update


def plain(tokens, d_all, ff_all, inputs, out_grad, weight, noise):
    w = weight.astype(BF16)
    x = lax.all_gather(inputs, "hidden", axis=0, tiled=True)
    g = lax.all_gather(out_grad, "mp", axis=0, tiled=True)
    clip = math.sqrt(SEQ * d_all * ff_all)
    outputs = lax.psum_scatter(
        jnp.dot(x, w, preferred_element_type=F32), "mp", scatter_dimension=0, tiled=True
    )
    in_grad = lax.psum_scatter(
        lax.dot_general(g, w, (((1,), (1,)), ((), ())), preferred_element_type=F32),
        "hidden",
        scatter_dimension=0,
        tiled=True,
    )
    grams = lax.psum(gram(x), "mp") * lax.psum(gram(g), "hidden")
    squares = jnp.maximum(jnp.sum(grams, axis=(1, 2)), 0.0)
    factor = jnp.minimum(1.0, clip / jnp.sqrt(squares + 1e-06))
    none = lambda at, j: 0
    update = make_update(
        jnp.zeros((1,), jnp.int32),
        [(x, None)],
        [g],
        none,
        none,
        jnp.repeat(factor, SEQ)[:, None],
        noise,
        math.sqrt(d_all * ff_all) / clip,
        tokens // SEQ,
    )
    return outputs.astype(BF16), in_grad.astype(BF16), update


def solution(mesh):
    mp, hidden = mesh.shape["mp"], mesh.shape["hidden"]

    def shards(inputs, out_grad, weight, noise):
        if mp == hidden == 4 and inputs.shape[0] % (2 * SEQ) == 0:
            return pipelined(inputs, out_grad, weight, noise)
        return plain(
            inputs.shape[0] * hidden,
            inputs.shape[1] * mp,
            out_grad.shape[1] * hidden,
            inputs,
            out_grad,
            weight,
            noise,
        )

    in_specs = (
        P(("groups", "hidden"), "mp"),
        P(("groups", "mp"), "hidden"),
        P("mp", "hidden"),
        P(None, ("groups", "mp"), "hidden"),
    )
    out_specs = (
        P(("groups", "mp"), "hidden"),
        P(("groups", "hidden"), "mp"),
        P("mp", ("groups", "hidden")),
    )
    return jax.shard_map(shards, mesh=mesh, in_specs=in_specs, out_specs=out_specs, check_vma=False)
```

```python
import math

import jax
import jax.numpy as jnp
from jax import lax
from jax.experimental import pallas as pl
from jax.experimental.pallas import tpu as pltpu
from jax.sharding import PartitionSpec as P

SEQ = 64
NOISE_BAND = 0.6
NOISE_SCALE = 4.0
VMEM = 63 * 1024 * 1024
F32 = jnp.float32
BF16 = jnp.bfloat16
ANY = pl.BlockSpec(memory_space=pl.ANY)
BRIEF = pl.CostEstimate(flops=1, bytes_accessed=1, transcendentals=0)


def params(dims):
    return pltpu.CompilerParams(
        vmem_limit_bytes=VMEM, dimension_semantics=("arbitrary",) * dims
    )


def whole(shape):
    return pl.BlockSpec(shape, lambda *_: (0,) * len(shape))


def pair_kernel(transposed, place, finish, count, merged, extra, keep, at, *refs):
    pieces, w = refs[:count], refs[count]
    merges = refs[count + 1 : count + 1 + merged]
    *products, rows = refs[count + 1 + merged + extra :]
    kept = products.pop() if keep else None
    r = rows.shape[0] // 2

    @pl.when(pl.program_id(0) == 0)
    def _():
        for cond, slot, spot, piece in place(at, pieces):

            def put(slot=slot, spot=spot, piece=piece):
                rows[pl.ds(pl.multiple_of(slot * r, r), r), :] = piece[...]
                if keep:
                    kept[spot] = piece[...]

            if cond is None:
                put()
            else:
                pl.when(cond)(put)

    tile = w[...]
    if tile.dtype != BF16:
        tile = tile.astype(BF16)
        products[-1][...] = tile
    dims = (((1,), (1 if transposed else 0,)), ((), ()))
    total = lax.dot_general(rows[...], tile, dims, preferred_element_type=F32)
    finish(at, total[:r], total[r:], merges, products)


def pair_matmul(
    at, pieces, w, place, transposed, finish, outs, merges, after, name, keep=False, share=(0, 8), before=()
):
    r, depth = pieces[0].shape
    width = w.shape[0] if transposed else w.shape[1]
    cast = w.dtype != BF16
    tile = min(256 if cast else 512 if transposed else 1024, width)
    skip = width // tile * share[0] // 8
    steps = width // tile * share[1] // 8 - skip
    w_spec = (
        pl.BlockSpec((tile, depth), lambda i: (i + skip, 0))
        if transposed
        else pl.BlockSpec((depth, tile), lambda i: (0, i + skip))
    )
    extra = [*before, *after]
    count = len(pieces)
    first_extra = count + 2 + len(merges)
    product = pl.BlockSpec((r, tile), lambda i: (0, i + skip))
    kernel = lambda *refs: pair_kernel(
        transposed, place, finish, count, len(merges), len(extra), keep, *refs
    )
    return pl.pallas_call(
        kernel,
        grid=(steps,),
        in_specs=[pl.BlockSpec(memory_space=pltpu.SMEM)]
        + [whole((r, depth))] * count
        + [w_spec]
        + [product] * len(merges)
        + [ANY] * len(extra),
        out_specs=[product] * outs + [w_spec] * cast + [whole((2, r, depth))] * keep,
        scratch_shapes=[pltpu.VMEM((2 * r, depth), BF16)],
        out_shape=[jax.ShapeDtypeStruct((r, width), BF16)] * outs
        + [jax.ShapeDtypeStruct(w.shape, BF16)] * cast
        + [jax.ShapeDtypeStruct((2, r, depth), BF16)] * keep,
        input_output_aliases={first_extra + i: i for i in range(len(before))},
        compiler_params=params(1),
        cost_estimate=BRIEF,
        name=name,
    )(at, *pieces, w, *merges, *extra)


def update_kernel(gain, count, nx, ng, extra, slot_of, block_of, at, factor, *refs):
    xs, gs, noise = refs[:nx], refs[nx : nx + ng], refs[nx + ng]
    out, scaled, rows = refs[nx + ng + 1 + extra :]
    rx, rg = rows.shape[0] // nx, scaled.shape[0] // ng

    @pl.when(pl.program_id(0) == 0)
    def _():
        for j, g in enumerate(gs):
            block = block_of(at, j)
            source, target = block * rg, slot_of(at, block) * rg
            for t in range(0, rg, SEQ):
                scale = factor[pl.ds(pl.multiple_of(source + t, SEQ), SEQ), :]
                scaled[pl.ds(pl.multiple_of(target + t, SEQ), SEQ), :] = (
                    g[t : t + SEQ, :].astype(F32) * scale
                ).astype(BF16)

    for j, x in enumerate(xs):
        rows[j * rx : (j + 1) * rx, :] = x[...].reshape(rx, -1)
    step = min(1024, out.shape[1])
    for j in range(0, out.shape[1], step):
        span = pl.ds(j, step)
        grad = lax.dot_general(
            rows[...], scaled[:, span], (((0,), (0,)), ((), ())), preferred_element_type=F32
        )
        band = noise[0, :, span].astype(F32) - NOISE_BAND * noise[1, :, span].astype(F32)
        out[:, span] = (grad * gain + NOISE_SCALE * band) * (1.0 / count)


def make_update(
    at, xs, gs, slot_of, block_of, factor, noise, gain, count, part=0, parts=1, before=None, after=()
):
    tokens = factor.shape[0]
    depth, whole_width = noise.shape[1:]
    width = whole_width // parts
    tile = min(512, depth)
    rx, rg = tokens // len(xs), tokens // len(gs)
    extra = ([] if before is None else [before]) + list(after)

    def x_spec(lead):
        if lead is None:
            return pl.BlockSpec((rx, tile), lambda i: (0, i))
        return pl.BlockSpec((1, rx, tile), lambda i: (lead, 0, i))

    def kernel(*refs):
        update_kernel(gain, count, len(xs), len(gs), len(extra), slot_of, block_of, *refs)

    return pl.pallas_call(
        kernel,
        grid=(depth // tile,),
        in_specs=[pl.BlockSpec(memory_space=pltpu.SMEM), whole((tokens, 1))]
        + [x_spec(lead) for _, lead in xs]
        + [pl.BlockSpec((rg, width), lambda i: (0, part))] * len(gs)
        + [pl.BlockSpec((2, tile, width), lambda i: (0, i, part))]
        + [ANY] * len(extra),
        out_specs=pl.BlockSpec((tile, width), lambda i: (i, part)),
        out_shape=jax.ShapeDtypeStruct((depth, whole_width), F32),
        scratch_shapes=[pltpu.VMEM((tokens, width), BF16), pltpu.VMEM((tokens, tile), BF16)],
        input_output_aliases={} if before is None else {3 + len(xs) + len(gs): 0},
        compiler_params=params(1),
        cost_estimate=BRIEF,
        name="update",
    )(at, factor, *[x for x, _ in xs], *gs, noise, *extra)


def add_kernel(sums, ins, at, *refs):
    sums(at, refs[:ins], refs[ins:])


def add_up(at, sums, arrays, choices, outs, steps, name):
    def band(shape, cond=None):
        def index(i, at):
            return (i if cond is None else jnp.where(cond(at), i, 0), 0)

        return pl.BlockSpec((shape[0] // steps, shape[1]), index)

    arrays, chosen = list(arrays), [x for _, x in choices]
    return pl.pallas_call(
        lambda *refs: add_kernel(sums, len(arrays) + len(chosen), *refs),
        grid_spec=pltpu.PrefetchScalarGridSpec(
            num_scalar_prefetch=1,
            grid=(steps,),
            in_specs=[band(x.shape) for x in arrays] + [band(x.shape, c) for c, x in choices],
            out_specs=[band(shape) for shape in outs],
        ),
        out_shape=[jax.ShapeDtypeStruct(shape, BF16) for shape in outs],
        compiler_params=params(1),
        cost_estimate=BRIEF,
        name=name,
    )(at, *arrays, *chosen)


def total(*refs):
    return sum(ref[...].astype(F32) for ref in refs)


OUTER = [(0, 1), (1, 0), (2, 3), (3, 2)]
INWARD = [(0, 1), (3, 2)]
OUTWARD = [(1, 0), (2, 3)]


def along(value, pairs):
    return lax.ppermute(value, "hidden", pairs)


def middle(value):
    pairs = [
        (m * 4 + h, m * 4 + 3 - h if h in (1, 2) else (m ^ 1) * 4 + h)
        for m in range(4)
        for h in range(4)
    ]
    return lax.ppermute(value, ("mp", "hidden"), pairs)


def swap(value, bit):
    return lax.ppermute(value, "mp", [(i, i ^ bit) for i in range(4)])


def gram(rows):
    blocks = rows.reshape(-1, SEQ, rows.shape[1])
    return jnp.einsum("bsd,btd->bst", blocks, blocks, preferred_element_type=F32)


def gram_kernel(*refs):
    *arrays, out = refs
    pairs = out.shape[0] // len(arrays)
    for i, rows in enumerate(arrays):
        for e in range(2 * pairs):
            block = rows[e * SEQ : (e + 1) * SEQ, :]
            square = lax.dot_general(
                block, block, (((1,), (1,)), ((), ())), preferred_element_type=F32
            )
            side = e % 2 * SEQ
            out[i * pairs + e // 2, :, side : side + SEQ] = square.astype(BF16)


def gram_pairs(*arrays):
    pairs = arrays[0].shape[0] // SEQ // 2
    return pl.pallas_call(
        gram_kernel,
        in_specs=[pl.BlockSpec(memory_space=pltpu.VMEM)] * len(arrays),
        out_specs=pl.BlockSpec(memory_space=pltpu.VMEM),
        out_shape=jax.ShapeDtypeStruct((len(arrays) * pairs, SEQ, 2 * SEQ), BF16),
        compiler_params=pltpu.CompilerParams(vmem_limit_bytes=VMEM),
        cost_estimate=BRIEF,
        name="gram",
    )(*arrays)


def factor_kernel(clip, pairs, n, at, *refs):
    *grams, out = refs
    h, m = at[2], at[3]
    r = out.shape[0] // n
    lane = lax.broadcasted_iota(jnp.int32, (1, 2 * SEQ), 1)
    for i, gram in enumerate(grams):
        block = m ^ i
        for p in range(pairs):
            spot = (block ^ h) * pairs + p
            feature = sum(g[spot].astype(F32) for g in grams)
            products = feature * gram[n * pairs + p].astype(F32)
            sums = jnp.sum(products, axis=0, keepdims=True)
            for side in range(2):
                square = jnp.sum(
                    jnp.where(lane // SEQ == side, sums, 0.0), axis=1, keepdims=True
                )
                factor = jnp.minimum(1.0, clip / jnp.sqrt(jnp.maximum(square, 0.0) + 1e-06))
                start = pl.multiple_of(block * r + (2 * p + side) * SEQ, SEQ)
                out[pl.ds(start, SEQ), :] = jnp.broadcast_to(factor, (SEQ, 1))


def make_factor(at, grams, clip, pairs, tokens):
    return pl.pallas_call(
        lambda *refs: factor_kernel(clip, pairs, len(grams), *refs),
        in_specs=[pl.BlockSpec(memory_space=pltpu.SMEM)]
        + [pl.BlockSpec(memory_space=pltpu.VMEM)] * len(grams),
        out_specs=pl.BlockSpec(memory_space=pltpu.VMEM),
        out_shape=jax.ShapeDtypeStruct((tokens, 1), F32),
        cost_estimate=BRIEF,
        name="clip_factor",
    )(at, *grams)


def plus(a, b):
    return (a.astype(F32) + b.astype(F32)).astype(BF16)


def pipelined(inputs, out_grad, weight, noise):
    n = 4
    m, h = lax.axis_index("mp"), lax.axis_index("hidden")
    at = jnp.stack([h // 2, m // 2, h, m]).astype(jnp.int32)
    d_all, ff_all = inputs.shape[1] * n, out_grad.shape[1] * n
    tokens = inputs.shape[0] * n
    clip = math.sqrt(SEQ * d_all * ff_all)
    hold = lax.optimization_barrier

    g_side = swap(out_grad, 1)
    g_far = swap(out_grad, 2)
    x_side = along(inputs, OUTER)
    x_mid = middle(inputs)
    grams = gram_pairs(inputs, out_grad)
    pairs = grams.shape[0] // 2
    features, units = grams[:pairs], grams[pairs:]
    weight, g_side, first_grams = hold((weight, g_side, grams))
    grams = along(grams, OUTER)


    def out_grad_rows(half):
        def place(at, pieces):
            core, near = at[3] & 1, half(at) == at[0]

            def slot(block_core):
                return jnp.where(near, (block_core ^ at[2] ^ 1) & 1, block_core ^ at[0] ^ 1)

            return [(None, slot(core), 0, pieces[0]), (None, slot(1 - core), 0, pieces[1])]

        return place

    def near_rows(at, pieces):
        slot = (at[2] ^ at[3]) & 1
        return [(None, slot, 0, pieces[0]), (None, 1 - slot, 0, pieces[1])]

    def far_rows(at, pieces):
        slot = (at[0] ^ at[3]) & 1
        inner = (at[2] == 1) | (at[2] == 2)
        outer = jnp.logical_not(inner)
        return [
            (inner, slot, 0, pieces[0]),
            (outer, slot, 0, pieces[1]),
            (inner, 1 - slot, 1, pieces[2]),
            (outer, 1 - slot, 1, pieces[3]),
        ]

    def plainly(at, first, second, merges, products):
        products[0][...] = first.astype(BF16)
        products[1][...] = second.astype(BF16)

    def in_grad_order(at, first, second, merges, products):
        near_first = at[0] == at[1]

        @pl.when(near_first)
        def _():
            products[0][...], products[1][...] = first.astype(BF16), second.astype(BF16)
            products[2][...], products[3][...] = merges[0][...], merges[1][...]

        @pl.when(jnp.logical_not(near_first))
        def _():
            products[0][...], products[1][...] = merges[0][...], merges[1][...]
            products[2][...], products[3][...] = first.astype(BF16), second.astype(BF16)

    def rows_here(share, before):
        return pair_matmul(
            at, [out_grad, g_side], weight, out_grad_rows(lambda at: at[1]), True, plainly, 2, [], [first_grams],
            "in_grad_here", share=share, before=before,
        )

    x_side, x_mid, grams, *qa = hold((x_side, x_mid, grams, *rows_here((0, 6), ())))
    x_mid2 = middle(x_side)
    x_out = along(x_mid, OUTER)
    qa0, qa1, w = rows_here((6, 8), qa)
    pa0, pa1 = pair_matmul(
        at, [inputs, x_side], w, near_rows, False, plainly, 2, [], [], "outputs_near"
    )
    g_far, pa1, x_mid2, x_out, grams = hold((g_far, pa1, x_mid2, x_out, grams))
    features = jnp.concatenate([features, grams[:pairs]])
    units = plus(units, grams[pairs:])
    grams = along(jnp.concatenate([features, units]), [(i, i ^ 2) for i in range(n)])
    g_far_side = swap(g_far, 1)
    x_out2 = along(x_mid2, OUTWARD)
    pa1 = swap(pa1, 1)
    first, second, beside, own = pair_matmul(
        at, [g_far, g_far_side], w, out_grad_rows(lambda at: 1 - at[1]), True, in_grad_order, 4,
        [qa0, qa1], [pa0], "in_grad_there",
    )
    grams, first, pa1 = hold((grams, first, pa1))
    grams = jnp.concatenate(
        [features, grams[: 2 * pairs], plus(units, grams[2 * pairs :])]
    )
    others = [swap(grams, j) for j in range(1, n)]
    r1a = along(first, INWARD)

    def two(at, refs, outs):
        outs[0][...] = total(*refs).astype(BF16)

    narrow, wide = first.shape, pa0.shape
    pb0, pb1, x_far = pair_matmul(
        at, [x_mid, x_out, x_mid2, x_out2], w, far_rows, False, plainly, 2,
        [], [first], "outputs_far", keep=True,
    )
    factor = make_factor(at, [grams, *others], clip, pairs, tokens)
    r1a, pb1, factor = hold((r1a, pb1, factor))
    pb1 = swap(pb1, 1)

    (r2a,) = add_up(at, two, [first, r1a], [], [narrow], 2, "sums_now")
    pb1, r2a = hold((pb1, r2a))
    r2a = middle(r2a)
    r1b = along(second, OUTER)

    def either(cond, pair, other):
        return jnp.where(cond, total(*pair), total(*other))

    def for_others(at, refs, outs):
        outs[0][...] = either(at[0] == at[1], refs[2:], refs[:2]).astype(BF16)

    def if_same(at):
        return at[0] == at[1]

    def if_other(at):
        return at[0] != at[1]

    (other,) = add_up(
        at, for_others, [], [(if_other, pa0), (if_other, pa1), (if_same, pb0), (if_same, pb1)],
        [wide], 2, "sums_others",
    )
    theirs = swap(other, 2)

    def inner_only(at, ref):
        return jnp.where((at[2] == 1) | (at[2] == 2), ref[...].astype(F32), 0.0)

    def later(at, refs, outs):
        outs[0][...] = (refs[0][...].astype(F32) + inner_only(at, refs[1])).astype(BF16)
        outs[1][...] = total(refs[2], refs[3]).astype(BF16)

    def last_outputs(at, refs, outs):
        mine = either(at[0] == at[1], refs[1:3], refs[3:])
        outs[0][...] = (mine + refs[0][...].astype(F32)).astype(BF16)

    def last_in_grad(at, refs, outs):
        outs[0][...] = (total(*refs[:2]) + inner_only(at, refs[2])).astype(BF16)

    def block_of(at, j):
        return at[3] ^ j

    def slot_of(at, block):
        far = jnp.where(at[0] == 0, block, 3 - block)
        return jnp.where(block // 2 == at[0], (block ^ at[2]) & 1, far)

    xs = [(inputs, None), (x_side, None), (x_far, 0), (x_far, 1)]
    gs = [out_grad, g_side, g_far, g_far_side]
    gain = math.sqrt(d_all * ff_all) / clip
    facts = (slot_of, block_of, factor, noise, gain, tokens // SEQ)
    update = make_update(at, xs, gs, *facts, 0, 2, None, [other])
    r2a, r1b, update = hold((r2a, r1b, update))
    r3, r2b = add_up(at, later, [beside, r2a, second, r1b], [], [narrow, narrow], 2, "sums_later")
    r3 = along(r3, OUTER)
    r2b = middle(r2b)
    update = make_update(at, xs, gs, *facts, 1, 2, update)
    theirs, update = hold((theirs, update))
    (outputs,) = add_up(
        at, last_outputs, [theirs],
        [(if_same, pa0), (if_same, pa1), (if_other, pb0), (if_other, pb1)], [wide], 2, "sums_outputs",
    )
    r3, r2b, outputs = hold((r3, r2b, outputs))
    (in_grad,) = add_up(at, last_in_grad, [own, r3, r2b], [], [narrow], 2, "sums_in_grad")
    return outputs, in_grad, update


def plain(tokens, d_all, ff_all, inputs, out_grad, weight, noise):
    w = weight.astype(BF16)
    x = lax.all_gather(inputs, "hidden", axis=0, tiled=True)
    g = lax.all_gather(out_grad, "mp", axis=0, tiled=True)
    clip = math.sqrt(SEQ * d_all * ff_all)
    outputs = lax.psum_scatter(
        jnp.dot(x, w, preferred_element_type=F32), "mp", scatter_dimension=0, tiled=True
    )
    in_grad = lax.psum_scatter(
        lax.dot_general(g, w, (((1,), (1,)), ((), ())), preferred_element_type=F32),
        "hidden",
        scatter_dimension=0,
        tiled=True,
    )
    grams = lax.psum(gram(x), "mp") * lax.psum(gram(g), "hidden")
    squares = jnp.maximum(jnp.sum(grams, axis=(1, 2)), 0.0)
    factor = jnp.minimum(1.0, clip / jnp.sqrt(squares + 1e-06))
    none = lambda at, j: 0
    update = make_update(
        jnp.zeros((1,), jnp.int32),
        [(x, None)],
        [g],
        none,
        none,
        jnp.repeat(factor, SEQ)[:, None],
        noise,
        math.sqrt(d_all * ff_all) / clip,
        tokens // SEQ,
    )
    return outputs.astype(BF16), in_grad.astype(BF16), update


def solution(mesh):
    mp, hidden = mesh.shape["mp"], mesh.shape["hidden"]

    def shards(inputs, out_grad, weight, noise):
        if mp == hidden == 4 and inputs.shape[0] % (2 * SEQ) == 0:
            return pipelined(inputs, out_grad, weight, noise)
        return plain(
            inputs.shape[0] * hidden,
            inputs.shape[1] * mp,
            out_grad.shape[1] * hidden,
            inputs,
            out_grad,
            weight,
            noise,
        )

    in_specs = (
        P(("groups", "hidden"), "mp"),
        P(("groups", "mp"), "hidden"),
        P("mp", "hidden"),
        P(None, ("groups", "mp"), "hidden"),
    )
    out_specs = (
        P(("groups", "mp"), "hidden"),
        P(("groups", "hidden"), "mp"),
        P("mp", ("groups", "hidden")),
    )
    return jax.shard_map(shards, mesh=mesh, in_specs=in_specs, out_specs=out_specs, check_vma=False)
```
